256 devices in a mesh: replica: 4 (over z_lo, core), fsdp: 64 (over y, z_hi, x).
Axes of the slice: x: 4, y: 4, z: 8 (z_hi: 4, z_lo: 2; z = z_hi * 2 + z_lo), core: 2. Of those that a mesh axis runs over, the one named last changes fastest.
Arguments:
- patches: bfloat16 [4, 49152, 6144], P('replica', 'fsdp'), may hold values from -6 to 6
- inner_weights: float32 [4, 6144, 256], P('replica', 'fsdp'), may hold values from -0.18 to 0.18
- inner_moment: float32 [4, 6144, 256], P('replica', 'fsdp'), may hold values from -0.0018 to 0.0018
- fragment_replica: bfloat16 [4, 4, 6144, 256], P('replica', None, 'fsdp'), may hold values from -0.1796875 to 0.1796875
- anchor: float32 [4, 6144, 256], P(None, 'fsdp'), may hold values from -0.18 to 0.18
- outer_moment: float32 [4, 6144, 256], P(None, 'fsdp'), may hold values from -0.12 to 0.12
- fragment_index: int32 [1], replicated, may hold values from 0 to 4095
Outputs:
- new_weights: float32 [4, 6144, 256], P('replica', 'fsdp')
- new_moment: float32 [4, 6144, 256], P('replica', 'fsdp')
- new_fragment: bfloat16 [4, 4, 6144, 256], P('replica', None, 'fsdp')
- new_anchor: float32 [4, 6144, 256], P(None, 'fsdp')
- new_outer_moment: float32 [4, 6144, 256], P(None, 'fsdp')
The draws below stay inside these ranges and needn't reach their ends.
All inputs are finite; a program needn't handle non-finite values.
Results may differ from the reference program's by a relative error of at most 0.027.
Values may be sent and summed in bfloat16 or wider, within the bound.
No kernel may reach another device: no remote copies, remote signals or barrier semaphores. Data moves between devices by JAX's collectives and lax.ppermute only.
A program may use at most 128 MiB of HBM per device.

```python
import jax
import jax.numpy as jnp
from jax import lax

D = 6144
HEAD = 128
IMAGE = 256
INNER = 2
FRAGS = 4
TOKENS = 49152
N_REPLICA = 4


def steps_of(key, shape, split, low, largest):
    gain = 1.0
    for dim, blocks in split:
        draws = jax.random.uniform(jax.random.fold_in(jax.random.fold_in(key, 6), dim), (blocks,), jnp.float32, low / len(split), largest / len(split))
        gain = gain * jnp.repeat(jnp.exp(draws), shape[dim] // blocks).reshape((-1,) + (1,) * (len(shape) - 1 - dim))
    return gain


def bell_draw(stream_key, shape, deviation, most, split=(), held_as=jnp.bfloat16):
    entries = deviation * jax.random.normal(stream_key, shape, jnp.float32)
    if split:
        entries = entries * steps_of(stream_key, shape, split, -0.22, 0.18)
    return jnp.clip(entries, -most, most).astype(held_as)


def setup_inputs(seed: int = 0) -> dict:
    splits = jax.random.split(jax.random.key(seed), 8)
    patches = bell_draw(splits[0], (N_REPLICA, TOKENS, D), 1.0, 6.0, ((0, 4), (1, 64)))
    inner_weights = bell_draw(splits[1], (N_REPLICA, D, 2 * HEAD), 0.03, 0.18, ((0, 4), (1, 64)), jnp.float32)
    inner_moment = bell_draw(splits[2], (N_REPLICA, D, 2 * HEAD), 0.0003, 0.0018, ((0, 4), (1, 64)), jnp.float32)
    fragment_replica = bell_draw(splits[3], (N_REPLICA, FRAGS, D, 2 * HEAD), 0.03, 0.1796875, ((0, 4), (2, 64)))
    anchor = bell_draw(splits[4], (FRAGS, D, 2 * HEAD), 0.03, 0.18, ((1, 64),), jnp.float32)
    outer_moment = bell_draw(splits[5], (FRAGS, D, 2 * HEAD), 0.02, 0.12, ((1, 64),), jnp.float32)
    fragment_index = jax.random.randint(splits[6], (1,), 0, 4096).astype(jnp.int32)
    return {"patches": patches, "inner_weights": inner_weights, "inner_moment": inner_moment, "fragment_replica": fragment_replica, "anchor": anchor, "outer_moment": outer_moment, "fragment_index": fragment_index}


def soft_sign(value):
    return value / jnp.sqrt(value * value + 1e-06)

def next_patch(inputs):
    images = inputs.reshape(-1, IMAGE, inputs.shape[1])
    return jnp.roll(images, -1, axis=1).reshape(inputs.shape)

def inner_steps(weights, moment, inputs):
    wanted_f = next_patch(inputs).astype(jnp.float32)
    inputs_f = inputs.astype(jnp.float32)
    for turn in range(INNER):
        rounded = weights.astype(jnp.bfloat16)
        value_part = rounded[:, :HEAD]
        output_part = rounded[:, HEAD:]
        head = jnp.dot(inputs, value_part, preferred_element_type=jnp.float32).astype(jnp.bfloat16)
        out = inputs_f + jnp.dot(head, output_part.T, preferred_element_type=jnp.float32)
        dout = ((out - wanted_f) / TOKENS).astype(jnp.bfloat16)
        dhead = jnp.dot(dout, output_part, preferred_element_type=jnp.float32).astype(jnp.bfloat16)
        grad_value = jnp.dot(inputs.T, dhead, preferred_element_type=jnp.float32)
        grad_output = jnp.dot(dout.T, head, preferred_element_type=jnp.float32)
        grad = jnp.concatenate([grad_value, grad_output], axis=1)
        mixed = 0.9 * moment + 0.1 * grad
        weights = weights * (1.0 - 0.01 * 0.1) - 0.01 * soft_sign(mixed)
        moment = 0.99 * moment + 0.01 * grad
    return (weights, moment)

def reference(patches, inner_weights, inner_moment, fragment_replica, anchor, outer_moment, fragment_index):
    weight_list = []
    moment_list = []
    for replica_id in range(N_REPLICA):
        new_w, new_m = inner_steps(inner_weights[replica_id], inner_moment[replica_id], patches[replica_id])
        weight_list.append(new_w)
        moment_list.append(new_m)
    which = (fragment_index[0] % FRAGS).astype(jnp.int32)
    anchor_f = lax.dynamic_index_in_dim(anchor, which, 0, keepdims=False)
    moment_f = lax.dynamic_index_in_dim(outer_moment, which, 0, keepdims=False)
    local_f = lax.dynamic_index_in_dim(fragment_replica, which, 1, keepdims=False)
    deltas = anchor_f[None] - local_f.astype(jnp.float32)
    mean = lax.optimization_barrier(jnp.sum(deltas, axis=0)) / N_REPLICA
    moment_new = 0.9 * moment_f + mean
    anchor_new = anchor_f - 0.7 * (mean + 0.9 * moment_new)
    merged = (0.5 * local_f.astype(jnp.float32) + 0.5 * anchor_new[None]).astype(jnp.bfloat16)
    new_fragment = lax.dynamic_update_index_in_dim(fragment_replica, merged, which, 1)
    new_anchor = lax.dynamic_update_index_in_dim(anchor, anchor_new, which, 0)
    new_outer_moment = lax.dynamic_update_index_in_dim(outer_moment, moment_new, which, 0)
    return (jnp.stack(weight_list), jnp.stack(moment_list), new_fragment, new_anchor, new_outer_moment)
```

```python
import jax
import jax.numpy as jnp
from jax import lax
from jax.experimental import pallas as pl
from jax.experimental.pallas import tpu as pltpu
from jax.sharding import PartitionSpec as P

IMAGE = 256
INNER = 2
FRAGS = 4
SIDE = 4
CHUNKS = 6
STRIDE = {"x": 1, "z": 4, "y": 16}


def coordinate(index, axis):
    return (index // STRIDE[axis]) % SIDE


def moved(value, axis, by):
    pairs = []
    for source in range(SIDE**3):
        place = coordinate(source, axis)
        pairs.append((source, source + ((place + by) % SIDE - place) * STRIDE[axis]))
    return lax.ppermute(value, "fsdp", pairs)


def soft_sign(value):
    return value / jnp.sqrt(value * value + 1e-06)


def row_offset(place, rx, ry, rz, rows):
    x = lax.rem(place[0] + rx, SIDE)
    y = lax.rem(place[1] + ry, SIDE)
    z = lax.rem(place[2] + rz, SIDE)
    return pl.multiple_of(((y * SIDE + z) * SIDE + x) * rows, 32)


def split_bf16(value):
    high = value.astype(jnp.bfloat16)
    low = (value - high.astype(jnp.float32)).astype(jnp.bfloat16)
    return high, low


def dot(a, b):
    return jnp.dot(a, b, preferred_element_type=jnp.float32)


def dot_first(a, b):
    return lax.dot_general(a, b, (((0,), (0,)), ((), ())), preferred_element_type=jnp.float32)


def turn_kernel(place_ref, inputs_hbm, *refs):
    value_in, output_in = refs[:4], refs[4:8]
    value_out, output_out = refs[8:12], refs[12:16]
    inputs, weights, product, mixed, grad, sems = refs[16:]
    tokens, width = inputs.shape
    step = width // CHUNKS
    rows, head = value_in[0].shape[2:]
    place = (place_ref[0], place_ref[1], place_ref[2])

    def fetch(c):
        part = pl.ds(c * step, step)
        return pltpu.make_async_copy(inputs_hbm.at[:, part], inputs.at[:, part], sems.at[c])

    for c in range(CHUNKS):
        fetch(c).start()
    for i in range(SIDE):
        for j in range(SIDE):
            for rz in range(SIDE):
                weights[pl.ds(row_offset(place, i, j, rz, rows), rows), :head] = value_in[i][j, rz]
                weights[pl.ds(row_offset(place, j, i, rz, rows), rows), head:] = output_in[i][j, rz]
    output_part = weights[:, head:]
    gram_high, gram_low = split_bf16(dot_first(output_part, output_part))
    for c in range(CHUNKS):
        fetch(c).wait()
        part = slice(c * step, (c + 1) * step)
        term = dot(inputs[:, part], weights[part, :])
        if c == 0:
            product[...] = term
        else:
            product[...] += term
    squares = jnp.zeros((head, head), jnp.float32)
    for image in range(tokens // IMAGE):
        span = slice(image * IMAGE, (image + 1) * IMAGE)
        rounded = product[span, :head].astype(jnp.bfloat16)
        projected = product[span, head:]
        following = pltpu.roll(projected, IMAGE - 1, 0)
        back = projected - following + dot(rounded, gram_high) + dot(rounded, gram_low)
        hidden = rounded.astype(jnp.float32)
        mixed[span, :head] = back.astype(jnp.bfloat16)
        mixed[span, head:] = (hidden - pltpu.roll(hidden, 1, 0)).astype(jnp.bfloat16)
        squares = squares + dot_first(rounded, rounded)
    squares_high, squares_low = split_bf16(squares)
    for c in range(CHUNKS):
        part = slice(c * step, (c + 1) * step)
        term = dot_first(inputs[:, part], mixed[...])
        output_rows = weights[part, head:]
        extra = dot(output_rows, squares_high) + dot(output_rows, squares_low)
        grad[part, :head] = term[:, :head].astype(jnp.bfloat16)
        grad[part, head:] = (term[:, head:] + extra).astype(jnp.bfloat16)
    for i in range(SIDE):
        for j in range(SIDE):
            for rz in range(SIDE):
                value_out[i][j, rz] = grad[pl.ds(row_offset(place, i, j, rz, rows), rows), :head]
                output_out[i][j, rz] = grad[pl.ds(row_offset(place, j, i, rz, rows), rows), head:]


def turn_call(place, inputs, value_parts, output_parts):
    tokens, width = inputs.shape
    shape = value_parts[0].shape
    head = shape[-1]
    out = jax.ShapeDtypeStruct(shape, jnp.bfloat16)
    vmem = pl.BlockSpec(memory_space=pltpu.VMEM)
    return pl.pallas_call(
        turn_kernel,
        out_shape=[out] * 8,
        in_specs=[pl.BlockSpec(memory_space=pltpu.SMEM), pl.BlockSpec(memory_space=pl.ANY)]
        + [vmem] * 8,
        out_specs=[vmem] * 8,
        scratch_shapes=[
            pltpu.VMEM((tokens, width), jnp.bfloat16),
            pltpu.VMEM((width, 2 * head), jnp.bfloat16),
            pltpu.VMEM((tokens, 2 * head), jnp.float32),
            pltpu.VMEM((tokens, 2 * head), jnp.bfloat16),
            pltpu.VMEM((width, 2 * head), jnp.bfloat16),
            pltpu.SemaphoreType.DMA((CHUNKS,)),
        ],
        compiler_params=pltpu.CompilerParams(vmem_limit_bytes=48 * 1024 * 1024),
        cost_estimate=pl.CostEstimate(
            flops=8 * tokens * width * head, bytes_accessed=2 * tokens * width, transcendentals=0
        ),
    )(place, inputs, *value_parts, *output_parts)


def gather_weights(rounded):
    head = rounded.shape[1] // 2
    column = jnp.stack([rounded] + [moved(rounded, "z", -k) for k in (1, 2, 3)])
    value, output = column[:, :, :head], column[:, :, head:]
    value = jnp.stack([value] + [moved(value, "y", -k) for k in (1, 2, 3)])
    output = jnp.stack([output] + [moved(output, "x", -k) for k in (1, 2, 3)])
    value_parts, output_parts = [value], [output]
    for k in (1, 2, 3):
        value_parts.append(moved(value, "x", -k))
        output_parts.append(moved(output, "y", -k))
    return value_parts, output_parts


def added(parts):
    total = parts[0].astype(jnp.float32)
    for part in parts[1:]:
        total = total + part.astype(jnp.float32)
    return total


def scatter_sum(value_parts, output_parts):
    value, output = [value_parts[0]], [output_parts[0]]
    for k in (1, 2, 3):
        value.append(moved(value_parts[k], "x", k))
        output.append(moved(output_parts[k], "y", k))
    value = added(value).astype(jnp.bfloat16)
    output = added(output).astype(jnp.bfloat16)
    value_next, output_next = [value[0]], [output[0]]
    for k in (1, 2, 3):
        value_next.append(moved(value[k], "y", k))
        output_next.append(moved(output[k], "x", k))
    both = jnp.concatenate([added(value_next), added(output_next)], axis=-1)
    rounded = both.astype(jnp.bfloat16)
    return added([both[0]] + [moved(rounded[k], "z", k) for k in (1, 2, 3)])


def inner_steps(weights, moment, inputs):
    tokens = inputs.shape[0] * lax.axis_size("fsdp")
    index = lax.axis_index("fsdp")
    place = jnp.stack([coordinate(index, axis) for axis in ("x", "y", "z")]).astype(jnp.int32)
    for turn in range(INNER):
        value_parts, output_parts = gather_weights(weights.astype(jnp.bfloat16))
        outs = turn_call(place, inputs, value_parts, output_parts)
        grad = scatter_sum(outs[:4], outs[4:]) * (1.0 / tokens)
        mixed = 0.9 * moment + 0.1 * grad
        weights = weights * (1.0 - 0.01 * 0.1) - 0.01 * soft_sign(mixed)
        moment = 0.99 * moment + 0.01 * grad
    return (weights, moment)


def outer_step(fragment_replica, anchor, outer_moment, fragment_index):
    which = fragment_index[0] % FRAGS
    anchor_f = lax.dynamic_index_in_dim(anchor, which, 0, keepdims=False)
    moment_f = lax.dynamic_index_in_dim(outer_moment, which, 0, keepdims=False)
    local_f = lax.dynamic_index_in_dim(fragment_replica[0], which, 0, keepdims=False)
    delta = anchor_f - local_f.astype(jnp.float32)
    replicas = lax.axis_size("replica")
    mean = lax.psum(delta, "replica") / replicas
    moment_new = 0.9 * moment_f + mean
    anchor_new = anchor_f - 0.7 * (mean + 0.9 * moment_new)
    merged = (0.5 * local_f.astype(jnp.float32) + 0.5 * anchor_new).astype(jnp.bfloat16)
    new_fragment = lax.dynamic_update_index_in_dim(fragment_replica[0], merged, which, 0)[None]
    new_anchor = lax.dynamic_update_index_in_dim(anchor, anchor_new, which, 0)
    new_outer_moment = lax.dynamic_update_index_in_dim(outer_moment, moment_new, which, 0)
    return (new_fragment, new_anchor, new_outer_moment)


def body(
    patches, inner_weights, inner_moment, fragment_replica, anchor, outer_moment, fragment_index
):
    weights, moment = inner_steps(inner_weights[0], inner_moment[0], patches[0])
    outer_result = outer_step(fragment_replica, anchor, outer_moment, fragment_index)
    new_fragment, new_anchor, new_outer_moment = outer_result
    return (weights[None], moment[None], new_fragment, new_anchor, new_outer_moment)


def solution(mesh):
    return jax.shard_map(
        body,
        mesh=mesh,
        in_specs=(
            P("replica", "fsdp", None),
            P("replica", "fsdp", None),
            P("replica", "fsdp", None),
            P("replica", None, "fsdp", None),
            P(None, "fsdp", None),
            P(None, "fsdp", None),
            P(),
        ),
        out_specs=(
            P("replica", "fsdp", None),
            P("replica", "fsdp", None),
            P("replica", None, "fsdp", None),
            P(None, "fsdp", None),
            P(None, "fsdp", None),
        ),
        check_vma=False,
    )
```

```python
import jax
import jax.numpy as jnp
from jax import lax
from jax.experimental import pallas as pl
from jax.experimental.pallas import tpu as pltpu
from jax.sharding import PartitionSpec as P

IMAGE = 256
INNER = 2
FRAGS = 4
REPLICAS = 4
SIDE = 4
CHUNKS = 6
STRIDE = {"x": 1, "z": 4, "y": 16}


def coordinate(index, axis):
    return (index // STRIDE[axis]) % SIDE


def near(place):
    return place + 1 - 2 * (place % 2)


def far(place):
    return SIDE - 1 - place


def near_first(place):
    return [place, near(place), far(place), near(far(place))]


def far_first(place):
    return [place, far(place), near(place), far(near(place))]


def sent(value, axis, to):
    pairs = []
    for source in range(SIDE**3):
        place = coordinate(source, axis)
        pairs.append((source, source + (to(place) - place) * STRIDE[axis]))
    return lax.ppermute(value, "fsdp", pairs)


def soft_sign(value):
    return value / jnp.sqrt(value * value + 1e-06)


def split_bf16(value):
    high = value.astype(jnp.bfloat16)
    low = (value - high.astype(jnp.float32)).astype(jnp.bfloat16)
    return high, low


def dot(a, b):
    return jnp.dot(a, b, preferred_element_type=jnp.float32)


def dot_first(a, b):
    return lax.dot_general(a, b, (((0,), (0,)), ((), ())), preferred_element_type=jnp.float32)


def blocks(table_ref, rows):
    found = []
    for part in range(4):
        output, back = part // 2, part % 2
        for i in range(SIDE):
            for j in range(SIDE // 2):
                for k in range(SIDE):
                    first = table_ref[2 * output + back, i]
                    second = table_ref[2 * (1 - output), 2 * back + j]
                    x, y = (second, first) if output else (first, second)
                    block = (y * SIDE + table_ref[4, k]) * SIDE + x
                    found.append((part, (i, j, k), pl.multiple_of(block * rows, 32), output))
    return found


def turn_kernel(table_ref, inputs_hbm, *refs):
    kept_in, other_in = refs[0:4], refs[4:8]
    kept_out, other_out = refs[8:12], refs[12:16]
    inputs, weights, product, mixed, grad, sems = refs[16:]
    tokens, width = inputs.shape
    step = width // CHUNKS
    rows, head = kept_in[0].shape[3:]
    places = blocks(table_ref, rows)

    def fetch(c):
        part = pl.ds(c * step, step)
        return pltpu.make_async_copy(inputs_hbm.at[:, part], inputs.at[:, part], sems.at[c])

    for c in range(CHUNKS):
        fetch(c).start()
    for part, (i, j, k), row, output in places:
        source = kept_in[part][i, j, k] if i < 2 else other_in[part][i - 2, j, k]
        weights[pl.ds(row, rows), output * head : (output + 1) * head] = source
    output_part = weights[:, head:]
    gram_high, gram_low = split_bf16(dot_first(output_part, output_part))
    for c in range(CHUNKS):
        fetch(c).wait()
        part = slice(c * step, (c + 1) * step)
        term = dot(inputs[:, part], weights[part, :])
        if c == 0:
            product[...] = term
        else:
            product[...] += term
    gram = jnp.concatenate([gram_high, gram_low], axis=0)
    squares = jnp.zeros((head, head), jnp.float32)
    for image in range(tokens // IMAGE):
        span = slice(image * IMAGE, (image + 1) * IMAGE)
        rounded = product[span, :head].astype(jnp.bfloat16)
        projected = product[span, head:]
        following = pltpu.roll(projected, IMAGE - 1, 0)
        twice = jnp.concatenate([rounded, rounded], axis=1)
        back = projected - following + dot(twice, gram)
        hidden = rounded.astype(jnp.float32)
        mixed[span, :head] = back.astype(jnp.bfloat16)
        mixed[span, head:] = (hidden - pltpu.roll(hidden, 1, 0)).astype(jnp.bfloat16)
        squares = squares + dot_first(rounded, rounded)
    squares = jnp.concatenate(split_bf16(squares), axis=0)
    for c in range(CHUNKS):
        part = slice(c * step, (c + 1) * step)
        term = dot_first(inputs[:, part], mixed[...])
        output_rows = weights[part, head:]
        extra = dot(jnp.concatenate([output_rows, output_rows], axis=1), squares)
        grad[part, :head] = term[:, :head].astype(jnp.bfloat16)
        grad[part, head:] = (term[:, head:] + extra).astype(jnp.bfloat16)
    for part, (i, j, k), row, output in places:
        block = grad[pl.ds(row, rows), output * head : (output + 1) * head]
        if i < 2:
            kept_out[part][i, j, k] = block
        else:
            other_out[part][i - 2, j, k] = block


def turn_call(table, inputs, kept, other):
    tokens, width = inputs.shape
    shape = kept[0].shape
    head = shape[-1]
    out = jax.ShapeDtypeStruct(shape, jnp.bfloat16)
    vmem = pl.BlockSpec(memory_space=pltpu.VMEM)
    outs = pl.pallas_call(
        turn_kernel,
        out_shape=[out] * 8,
        in_specs=[pl.BlockSpec(memory_space=pltpu.SMEM), pl.BlockSpec(memory_space=pl.ANY)]
        + [vmem] * 8,
        out_specs=[vmem] * 8,
        scratch_shapes=[
            pltpu.VMEM((tokens, width), jnp.bfloat16),
            pltpu.VMEM((width, 2 * head), jnp.bfloat16),
            pltpu.VMEM((tokens, 2 * head), jnp.float32),
            pltpu.VMEM((tokens, 2 * head), jnp.bfloat16),
            pltpu.VMEM((width, 2 * head), jnp.bfloat16),
            pltpu.SemaphoreType.DMA((CHUNKS,)),
        ],
        compiler_params=pltpu.CompilerParams(vmem_limit_bytes=36 * 1024 * 1024),
        cost_estimate=pl.CostEstimate(
            flops=8 * tokens * width * head, bytes_accessed=2 * tokens * width, transcendentals=0
        ),
    )(table, inputs, *kept, *other)
    return outs[:4], outs[4:]


WAYS = ((near, far), (far, near), (near, far), (far, near))
AXES = ("x", "x", "y", "y")


def gather_columns(rounded):
    head = rounded.shape[1] // 2
    parts = [rounded]
    for k in range(1, SIDE):
        parts.append(sent(rounded, "z", lambda place, k=k: (place - k) % SIDE))
    column = jnp.stack(parts)
    halves = [column[:, :, :head], column[:, :, head:]]
    pairs = [jnp.stack([h, sent(h, axis, near)]) for h, axis in zip(halves, ("y", "x"))]
    return [jnp.concatenate([p, sent(p, axis, far)]) for p, axis in zip(pairs, ("y", "x"))]


def gather_rest(wide):
    parts = [wide[0][:2], wide[0][2:], wide[1][:2], wide[1][2:]]
    first = [sent(p, axis, way[0]) for p, axis, way in zip(parts, AXES, WAYS)]
    kept = [jnp.stack(both) for both in zip(parts, first)]
    other = [sent(p, axis, way[1]) for p, axis, way in zip(kept, AXES, WAYS)]
    return kept, other


def scatter_first(kept, other):
    got = [sent(p, axis, way[1]) for p, axis, way in zip(other, AXES, WAYS)]
    sums = [a.astype(jnp.float32) + b.astype(jnp.float32) for a, b in zip(kept, got)]
    got = [
        sent(s[1].astype(jnp.bfloat16), axis, way[0]) for s, axis, way in zip(sums, AXES, WAYS)
    ]
    return [s[0] + b.astype(jnp.float32) for s, b in zip(sums, got)]


def scatter_rest(parts):
    columns = []
    for half, axis in ((0, "y"), (1, "x")):
        got = sent(parts[2 * half + 1].astype(jnp.bfloat16), axis, far)
        pair = parts[2 * half] + got.astype(jnp.float32)
        got = sent(pair[1].astype(jnp.bfloat16), axis, near)
        columns.append(pair[0] + got.astype(jnp.float32))
    column = jnp.concatenate(columns, axis=-1)
    rounded = column.astype(jnp.bfloat16)
    total = column[0]
    for k in range(1, SIDE):
        got = sent(rounded[k], "z", lambda place, k=k: (place + k) % SIDE)
        total = total + got.astype(jnp.float32)
    return total


def outer_sum(anchor_f, local_f):
    partner = lax.ppermute(local_f, "replica", [(0, 1), (1, 0), (2, 3), (3, 2)])
    pair = (anchor_f - local_f.astype(jnp.float32)) + (anchor_f - partner.astype(jnp.float32))
    return pair + lax.ppermute(pair, "replica", [(0, 2), (2, 0), (1, 3), (3, 1)])


def outer_kernel(which_ref, fragment, anchor, moment, total, new_fragment, new_anchor, new_moment):
    which = which_ref[0]
    new_fragment[...] = fragment[...]
    new_anchor[...] = anchor[...]
    new_moment[...] = moment[...]
    mean = total[...] * (1.0 / REPLICAS)
    moved = 0.9 * moment[which] + mean
    stepped = anchor[which] - 0.7 * (mean + 0.9 * moved)
    new_moment[which] = moved
    new_anchor[which] = stepped
    local = fragment[which].astype(jnp.float32)
    new_fragment[which] = (0.5 * local + 0.5 * stepped).astype(jnp.bfloat16)


def outer_call(which, fragment, anchor, moment, total):
    vmem = pl.BlockSpec(memory_space=pltpu.VMEM)
    return pl.pallas_call(
        outer_kernel,
        out_shape=[jax.ShapeDtypeStruct(a.shape, a.dtype) for a in (fragment, anchor, moment)],
        in_specs=[pl.BlockSpec(memory_space=pltpu.SMEM)] + [vmem] * 4,
        out_specs=[vmem] * 3,
        cost_estimate=pl.CostEstimate(flops=0, bytes_accessed=3 * 1024 * 1024, transcendentals=0),
    )(which, fragment, anchor, moment, total)


def label_table():
    index = lax.axis_index("fsdp")
    x, y, z = (coordinate(index, axis) for axis in ("x", "y", "z"))
    table = [near_first(x), far_first(x), near_first(y), far_first(y)]
    table.append([(z + k) % SIDE for k in range(SIDE)])
    return jnp.stack([jnp.stack(row) for row in table]).astype(jnp.int32)


def body(
    patches, inner_weights, inner_moment, fragment_replica, anchor, outer_moment, fragment_index
):
    inputs, weights, moment = patches[0], inner_weights[0], inner_moment[0]
    fragment = fragment_replica[0]
    tokens = inputs.shape[0] * lax.axis_size("fsdp")
    table = label_table()
    which = fragment_index % FRAGS
    total = outer = None
    for turn in range(INNER):
        wide = gather_columns(weights.astype(jnp.bfloat16))
        if turn == 0:
            wide, fragment, anchor, which = lax.optimization_barrier(
                (wide, fragment, anchor, which)
            )
            anchor_f = lax.dynamic_index_in_dim(anchor, which[0], 0, keepdims=False)
            local_f = lax.dynamic_index_in_dim(fragment, which[0], 0, keepdims=False)
            total = outer_sum(anchor_f, local_f)
        elif turn == 1:
            outer = outer_call(which, fragment, anchor, outer_moment, total)
            wide, outer = lax.optimization_barrier((wide, outer))
        kept, other = gather_rest(wide)
        kept, other = turn_call(table, inputs, kept, other)
        if turn == 0:
            kept, other, total = lax.optimization_barrier((kept, other, total))
        grad = scatter_rest(scatter_first(kept, other)) * (1.0 / tokens)
        mixed = 0.9 * moment + 0.1 * grad
        weights = weights * (1.0 - 0.01 * 0.1) - 0.01 * soft_sign(mixed)
        moment = 0.99 * moment + 0.01 * grad
    new_fragment, new_anchor, new_outer_moment = outer
    return (weights[None], moment[None], new_fragment[None], new_anchor, new_outer_moment)


def solution(mesh):
    return jax.shard_map(
        body,
        mesh=mesh,
        in_specs=(
            P("replica", "fsdp", None),
            P("replica", "fsdp", None),
            P("replica", "fsdp", None),
            P("replica", None, "fsdp", None),
            P(None, "fsdp", None),
            P(None, "fsdp", None),
            P(),
        ),
        out_specs=(
            P("replica", "fsdp", None),
            P("replica", "fsdp", None),
            P("replica", None, "fsdp", None),
            P(None, "fsdp", None),
            P(None, "fsdp", None),
        ),
        check_vma=False,
    )
```

```python
import jax
import jax.numpy as jnp
from jax import lax
from jax.experimental import pallas as pl
from jax.experimental.pallas import tpu as pltpu
from jax.sharding import PartitionSpec as P

IMAGE = 256
INNER = 2
FRAGS = 4
REPLICAS = 4
SIDE = 4
CHUNKS = 6
STRIDE = {"x": 1, "z": 4, "y": 16}


def coordinate(index, axis):
    return (index // STRIDE[axis]) % SIDE


def near(place):
    return place + 1 - 2 * (place % 2)


def far(place):
    return SIDE - 1 - place


def near_first(place):
    return [place, near(place), far(place), near(far(place))]


def far_first(place):
    return [place, far(place), near(place), far(near(place))]


def sent(value, axis, to):
    pairs = []
    for source in range(SIDE**3):
        place = coordinate(source, axis)
        pairs.append((source, source + (to(place) - place) * STRIDE[axis]))
    return lax.ppermute(value, "fsdp", pairs)


def soft_sign(value):
    return value / jnp.sqrt(value * value + 1e-06)


def split_bf16(value):
    high = value.astype(jnp.bfloat16)
    low = (value - high.astype(jnp.float32)).astype(jnp.bfloat16)
    return high, low


def dot(a, b):
    return jnp.dot(a, b, preferred_element_type=jnp.float32)


def dot_first(a, b):
    return lax.dot_general(a, b, (((0,), (0,)), ((), ())), preferred_element_type=jnp.float32)


def blocks(table_ref, rows):
    found = []
    for part in range(4):
        output, back = part // 2, part % 2
        for i in range(SIDE):
            for j in range(SIDE // 2):
                for k in range(SIDE):
                    first = table_ref[2 * output + back, i]
                    second = table_ref[2 * (1 - output), 2 * back + j]
                    x, y = (second, first) if output else (first, second)
                    block = (y * SIDE + table_ref[4, k]) * SIDE + x
                    found.append((part, (i, j, k), pl.multiple_of(block * rows, 32), output))
    return found


def turn_kernel(table_ref, inputs_hbm, *refs):
    kept_in, other_in = refs[0:4], refs[4:8]
    kept_out, other_out = refs[8:12], refs[12:16]
    inputs, weights, product, mixed, grad, sems = refs[16:]
    tokens, width = inputs.shape
    step = width // CHUNKS
    rows, head = kept_in[0].shape[3:]
    places = blocks(table_ref, rows)

    def fetch(c):
        part = pl.ds(pl.multiple_of(c * step, step), step)
        return pltpu.make_async_copy(inputs_hbm.at[:, part], inputs.at[:, part], sems.at[c])

    for c in range(CHUNKS):
        fetch(c).start()
    for part, (i, j, k), row, output in places:
        source = kept_in[part][i, j, k] if i < 2 else other_in[part][i - 2, j, k]
        weights[pl.ds(row, rows), output * head : (output + 1) * head] = source
    output_part = weights[:, head:]
    gram_high, gram_low = split_bf16(dot_first(output_part, output_part))
    product[...] = jnp.zeros_like(product)

    @pl.loop(0, CHUNKS)
    def _(c):
        fetch(c).wait()
        part = pl.ds(pl.multiple_of(c * step, step), step)
        product[...] += dot(inputs[:, part], weights[part, :])

    gram = jnp.concatenate([gram_high, gram_low], axis=0)
    squares = jnp.zeros((head, head), jnp.float32)
    for image in range(tokens // IMAGE):
        span = slice(image * IMAGE, (image + 1) * IMAGE)
        rounded = product[span, :head].astype(jnp.bfloat16)
        projected = product[span, head:]
        following = pltpu.roll(projected, IMAGE - 1, 0)
        twice = jnp.concatenate([rounded, rounded], axis=1)
        back = projected - following + dot(twice, gram)
        hidden = rounded.astype(jnp.float32)
        mixed[span, :head] = back.astype(jnp.bfloat16)
        mixed[span, head:] = (hidden - pltpu.roll(hidden, 1, 0)).astype(jnp.bfloat16)
        squares = squares + dot_first(rounded, rounded)
    squares = jnp.concatenate(split_bf16(squares), axis=0)

    @pl.loop(0, CHUNKS)
    def _(c):
        part = pl.ds(pl.multiple_of(c * step, step), step)
        term = dot_first(inputs[:, part], mixed[...])
        output_rows = weights[part, head:]
        extra = dot(jnp.concatenate([output_rows, output_rows], axis=1), squares)
        grad[part, :head] = term[:, :head].astype(jnp.bfloat16)
        grad[part, head:] = (term[:, head:] + extra).astype(jnp.bfloat16)

    for part, (i, j, k), row, output in places:
        block = grad[pl.ds(row, rows), output * head : (output + 1) * head]
        if i < 2:
            kept_out[part][i, j, k] = block
        else:
            other_out[part][i - 2, j, k] = block


def turn_call(table, inputs, kept, other):
    tokens, width = inputs.shape
    shape = kept[0].shape
    head = shape[-1]
    out = jax.ShapeDtypeStruct(shape, jnp.bfloat16)
    vmem = pl.BlockSpec(memory_space=pltpu.VMEM)
    outs = pl.pallas_call(
        turn_kernel,
        out_shape=[out] * 8,
        in_specs=[pl.BlockSpec(memory_space=pltpu.SMEM), pl.BlockSpec(memory_space=pl.ANY)]
        + [vmem] * 8,
        out_specs=[vmem] * 8,
        scratch_shapes=[
            pltpu.VMEM((tokens, width), jnp.bfloat16),
            pltpu.VMEM((width, 2 * head), jnp.bfloat16),
            pltpu.VMEM((tokens, 2 * head), jnp.float32),
            pltpu.VMEM((tokens, 2 * head), jnp.bfloat16),
            pltpu.VMEM((width, 2 * head), jnp.bfloat16),
            pltpu.SemaphoreType.DMA((CHUNKS,)),
        ],
        compiler_params=pltpu.CompilerParams(vmem_limit_bytes=48 * 1024 * 1024),
        cost_estimate=pl.CostEstimate(
            flops=8 * tokens * width * head, bytes_accessed=2 * tokens * width, transcendentals=0
        ),
    )(table, inputs, *kept, *other)
    return outs[:4], outs[4:]


WAYS = ((near, far), (far, near), (near, far), (far, near))
AXES = ("x", "x", "y", "y")


def gather_columns(rounded):
    head = rounded.shape[1] // 2
    parts = [rounded]
    for k in range(1, SIDE):
        parts.append(sent(rounded, "z", lambda place, k=k: (place - k) % SIDE))
    column = jnp.stack(parts)
    halves = [column[:, :, :head], column[:, :, head:]]
    pairs = [jnp.stack([h, sent(h, axis, near)]) for h, axis in zip(halves, ("y", "x"))]
    return [jnp.concatenate([p, sent(p, axis, far)]) for p, axis in zip(pairs, ("y", "x"))]


def gather_rest(wide):
    parts = [wide[0][:2], wide[0][2:], wide[1][:2], wide[1][2:]]
    first = [sent(p, axis, way[0]) for p, axis, way in zip(parts, AXES, WAYS)]
    kept = [jnp.stack(both) for both in zip(parts, first)]
    other = [sent(p, axis, way[1]) for p, axis, way in zip(kept, AXES, WAYS)]
    return kept, other


def scatter_first(kept, other, pair=None):
    got = [sent(p, axis, way[1]) for p, axis, way in zip(other, AXES, WAYS)]
    rest = None
    if pair is not None:
        rest = lax.ppermute(pair, "replica", [(0, 2), (2, 0), (1, 3), (3, 1)])
        got[3], rest = lax.optimization_barrier((got[3], rest))
    sums = [a.astype(jnp.float32) + b.astype(jnp.float32) for a, b in zip(kept, got)]
    got = [
        sent(s[1].astype(jnp.bfloat16), axis, way[0]) for s, axis, way in zip(sums, AXES, WAYS)
    ]
    return [s[0] + b.astype(jnp.float32) for s, b in zip(sums, got)], rest


def scatter_rest(parts):
    columns = []
    for half, axis in ((0, "y"), (1, "x")):
        got = sent(parts[2 * half + 1].astype(jnp.bfloat16), axis, far)
        pair = parts[2 * half] + got.astype(jnp.float32)
        got = sent(pair[1].astype(jnp.bfloat16), axis, near)
        columns.append(pair[0] + got.astype(jnp.float32))
    column = jnp.concatenate(columns, axis=-1)
    rounded = column.astype(jnp.bfloat16)
    total = column[0]
    for k in range(1, SIDE):
        got = sent(rounded[k], "z", lambda place, k=k: (place + k) % SIDE)
        total = total + got.astype(jnp.float32)
    return total


def replica_sum(anchor, fragment, which, after, before):
    after, anchor, fragment = lax.optimization_barrier((after, anchor, fragment))
    anchor_f = lax.dynamic_index_in_dim(anchor, which[0], 0, keepdims=False)
    local_f = lax.dynamic_index_in_dim(fragment, which[0], 0, keepdims=False)
    partner = lax.ppermute(local_f, "replica", [(0, 1), (1, 0), (2, 3), (3, 2)])
    before, partner = lax.optimization_barrier((before, partner))
    pair = (anchor_f - local_f.astype(jnp.float32)) + (anchor_f - partner.astype(jnp.float32))
    return pair, after, before


def outer_kernel(which_ref, fragment, anchor, moment, pair, rest, *outs):
    new_fragment, new_anchor, new_moment = outs
    which = which_ref[0]
    new_fragment[...] = fragment[...]
    new_anchor[...] = anchor[...]
    new_moment[...] = moment[...]
    mean = (pair[...] + rest[...]) * (1.0 / REPLICAS)
    moved = 0.9 * moment[which] + mean
    stepped = anchor[which] - 0.7 * (mean + 0.9 * moved)
    new_moment[which] = moved
    new_anchor[which] = stepped
    local = fragment[which].astype(jnp.float32)
    new_fragment[which] = (0.5 * local + 0.5 * stepped).astype(jnp.bfloat16)


def outer_call(which, fragment, anchor, moment, pair, rest):
    vmem = pl.BlockSpec(memory_space=pltpu.VMEM)
    return pl.pallas_call(
        outer_kernel,
        out_shape=[jax.ShapeDtypeStruct(a.shape, a.dtype) for a in (fragment, anchor, moment)],
        in_specs=[pl.BlockSpec(memory_space=pltpu.SMEM)] + [vmem] * 5,
        out_specs=[vmem] * 3,
        cost_estimate=pl.CostEstimate(flops=0, bytes_accessed=3 * 1024 * 1024, transcendentals=0),
    )(which, fragment, anchor, moment, pair, rest)


def label_table():
    index = lax.axis_index("fsdp")
    x, y, z = (coordinate(index, axis) for axis in ("x", "y", "z"))
    table = [near_first(x), far_first(x), near_first(y), far_first(y)]
    table.append([(z + k) % SIDE for k in range(SIDE)])
    return jnp.stack([jnp.stack(row) for row in table]).astype(jnp.int32)


def body(
    patches, inner_weights, inner_moment, fragment_replica, anchor, outer_moment, fragment_index
):
    inputs, weights, moment = patches[0], inner_weights[0], inner_moment[0]
    fragment = fragment_replica[0]
    tokens = inputs.shape[0] * lax.axis_size("fsdp")
    table = label_table()
    which = fragment_index % FRAGS
    rest = outer = None
    for turn in range(INNER):
        kept, other = gather_rest(gather_columns(weights.astype(jnp.bfloat16)))
        if turn == 0:
            pair, other[0], other[3] = replica_sum(anchor, fragment, which, other[0], other[3])
        else:
            other[0], pair = lax.optimization_barrier((other[0], pair))
            outer = outer_call(which, fragment, anchor, outer_moment, pair, rest)
            other[3], outer = lax.optimization_barrier((other[3], outer))
        kept, other = turn_call(table, inputs, kept, other)
        if turn == 0:
            kept, pair = lax.optimization_barrier((kept, pair))
            parts, rest = scatter_first(kept, other, pair)
        else:
            parts, _ = scatter_first(kept, other)
        grad = scatter_rest(parts) * (1.0 / tokens)
        mixed = 0.9 * moment + 0.1 * grad
        weights = weights * (1.0 - 0.01 * 0.1) - 0.01 * soft_sign(mixed)
        moment = 0.99 * moment + 0.01 * grad
    new_fragment, new_anchor, new_outer_moment = outer
    return (weights[None], moment[None], new_fragment[None], new_anchor, new_outer_moment)


def solution(mesh):
    return jax.shard_map(
        body,
        mesh=mesh,
        in_specs=(
            P("replica", "fsdp", None),
            P("replica", "fsdp", None),
            P("replica", "fsdp", None),
            P("replica", None, "fsdp", None),
            P(None, "fsdp", None),
            P(None, "fsdp", None),
            P(),
        ),
        out_specs=(
            P("replica", "fsdp", None),
            P("replica", "fsdp", None),
            P("replica", None, "fsdp", None),
            P(None, "fsdp", None),
            P(None, "fsdp", None),
        ),
        check_vma=False,
    )
```

```python
import jax
import jax.numpy as jnp
from jax import lax
from jax.experimental import pallas as pl
from jax.experimental.pallas import tpu as pltpu
from jax.sharding import PartitionSpec as P

IMAGE = 256
INNER = 2
FRAGS = 4
REPLICAS = 4
CORES = 2
DISTANCES = (0, 1, 3, 2)
SIDE = 4
CHUNKS = 6
STRIDE = {"x": 1, "z": 4, "y": 16}


def coordinate(index, axis):
    return (index // STRIDE[axis]) % SIDE


def near(place):
    return place + 1 - 2 * (place % 2)


def far(place):
    return SIDE - 1 - place


def near_first(place):
    return [place, near(place), far(place), near(far(place))]


def far_first(place):
    return [place, far(place), near(place), far(near(place))]


def axis_of(name, replica):
    if name == "z":
        return name
    return "x" if (name == "a") == (replica % CORES == 0) else "y"


def along_z(place, distance, core):
    return (place + distance if core == 0 else place - distance) % SIDE


def sent(value, axis, to):
    pairs = []
    for replica in range(REPLICAS):
        real = axis_of(axis, replica)
        for source in range(SIDE**3):
            place = coordinate(source, real)
            goal = along_z(place, to, replica % CORES) if axis == "z" else to(place)
            target = source + (goal - place) * STRIDE[real]
            pairs.append((replica * SIDE**3 + source, replica * SIDE**3 + target))
    return lax.ppermute(value, ("replica", "fsdp"), pairs)


def soft_sign(value):
    return value / jnp.sqrt(value * value + 1e-06)


def split_bf16(value):
    high = value.astype(jnp.bfloat16)
    low = (value - high.astype(jnp.float32)).astype(jnp.bfloat16)
    return high, low


def dot(a, b):
    return jnp.dot(a, b, preferred_element_type=jnp.float32)


def dot_first(a, b):
    return lax.dot_general(a, b, (((0,), (0,)), ((), ())), preferred_element_type=jnp.float32)


def blocks(table_ref, rows):
    found = []
    for part in range(4):
        output, back = part // 2, part % 2
        for i in range(SIDE):
            for j in range(SIDE // 2):
                for k in range(SIDE):
                    first = table_ref[2 * output + back, i]
                    second = table_ref[2 * (1 - output), 2 * back + j]
                    block = first + second + table_ref[4, k]
                    found.append((part, (i, j, k), pl.multiple_of(block * rows, 32), output))
    return found


def turn_kernel(table_ref, inputs_hbm, *refs):
    kept_in, other_in = refs[0:4], refs[4:8]
    kept_out, other_out = refs[8:12], refs[12:16]
    inputs, weights, product, mixed, grad, sems = refs[16:]
    tokens, width = inputs.shape
    step = width // CHUNKS
    rows, head = kept_in[0].shape[3:]
    places = blocks(table_ref, rows)

    def fetch(c):
        part = pl.ds(pl.multiple_of(c * step, step), step)
        return pltpu.make_async_copy(inputs_hbm.at[:, part], inputs.at[:, part], sems.at[c])

    for c in range(CHUNKS):
        fetch(c).start()
    for part, (i, j, k), row, output in places:
        source = kept_in[part][i, j, k] if i < 2 else other_in[part][i - 2, j, k]
        weights[pl.ds(row, rows), output * head : (output + 1) * head] = source
    output_part = weights[:, head:]
    gram_high, gram_low = split_bf16(dot_first(output_part, output_part))
    product[...] = jnp.zeros_like(product)

    @pl.loop(0, CHUNKS)
    def _(c):
        fetch(c).wait()
        part = pl.ds(pl.multiple_of(c * step, step), step)
        product[...] += dot(inputs[:, part], weights[part, :])

    gram = jnp.concatenate([gram_high, gram_low], axis=0)
    squares = jnp.zeros((head, head), jnp.float32)
    for image in range(tokens // IMAGE):
        span = slice(image * IMAGE, (image + 1) * IMAGE)
        rounded = product[span, :head].astype(jnp.bfloat16)
        projected = product[span, head:]
        following = pltpu.roll(projected, IMAGE - 1, 0)
        twice = jnp.concatenate([rounded, rounded], axis=1)
        back = projected - following + dot(twice, gram)
        hidden = rounded.astype(jnp.float32)
        mixed[span, :head] = back.astype(jnp.bfloat16)
        mixed[span, head:] = (hidden - pltpu.roll(hidden, 1, 0)).astype(jnp.bfloat16)
        squares = squares + dot_first(rounded, rounded)
    squares = jnp.concatenate(split_bf16(squares), axis=0)

    @pl.loop(0, CHUNKS)
    def _(c):
        part = pl.ds(pl.multiple_of(c * step, step), step)
        term = dot_first(inputs[:, part], mixed[...])
        output_rows = weights[part, head:]
        extra = dot(jnp.concatenate([output_rows, output_rows], axis=1), squares)
        grad[part, :head] = term[:, :head].astype(jnp.bfloat16)
        grad[part, head:] = (term[:, head:] + extra).astype(jnp.bfloat16)

    for part, (i, j, k), row, output in places:
        block = grad[pl.ds(row, rows), output * head : (output + 1) * head]
        if i < 2:
            kept_out[part][i, j, k] = block
        else:
            other_out[part][i - 2, j, k] = block


def turn_call(table, inputs, kept, other):
    tokens, width = inputs.shape
    shape = kept[0].shape
    head = shape[-1]
    out = jax.ShapeDtypeStruct(shape, jnp.bfloat16)
    vmem = pl.BlockSpec(memory_space=pltpu.VMEM)
    outs = pl.pallas_call(
        turn_kernel,
        out_shape=[out] * 8,
        in_specs=[pl.BlockSpec(memory_space=pltpu.SMEM), pl.BlockSpec(memory_space=pl.ANY)]
        + [vmem] * 8,
        out_specs=[vmem] * 8,
        scratch_shapes=[
            pltpu.VMEM((tokens, width), jnp.bfloat16),
            pltpu.VMEM((width, 2 * head), jnp.bfloat16),
            pltpu.VMEM((tokens, 2 * head), jnp.float32),
            pltpu.VMEM((tokens, 2 * head), jnp.bfloat16),
            pltpu.VMEM((width, 2 * head), jnp.bfloat16),
            pltpu.SemaphoreType.DMA((CHUNKS,)),
        ],
        compiler_params=pltpu.CompilerParams(vmem_limit_bytes=48 * 1024 * 1024),
        cost_estimate=pl.CostEstimate(
            flops=8 * tokens * width * head, bytes_accessed=2 * tokens * width, transcendentals=0
        ),
    )(table, inputs, *kept, *other)
    return outs[:4], outs[4:]


WAYS = ((near, far), (far, near), (near, far), (far, near))
AXES = ("a", "a", "b", "b")


def gather_columns(rounded):
    head = rounded.shape[1] // 2
    column = jnp.stack([rounded] + [sent(rounded, "z", -k) for k in DISTANCES[1:]])
    halves = [column[:, :, :head], column[:, :, head:]]
    pairs = [jnp.stack([h, sent(h, axis, near)]) for h, axis in zip(halves, ("b", "a"))]
    return [jnp.concatenate([p, sent(p, axis, far)]) for p, axis in zip(pairs, ("b", "a"))]


def gather_rest(wide):
    parts = [wide[0][:2], wide[0][2:], wide[1][:2], wide[1][2:]]
    first = [sent(p, axis, way[0]) for p, axis, way in zip(parts, AXES, WAYS)]
    kept = [jnp.stack(both) for both in zip(parts, first)]
    other = [sent(p, axis, way[1]) for p, axis, way in zip(kept, AXES, WAYS)]
    return kept, other


def scatter_first(kept, other, pair=None):
    got = [sent(p, axis, way[1]) for p, axis, way in zip(other, AXES, WAYS)]
    rest = None
    if pair is not None:
        rest = lax.ppermute(pair, "replica", [(0, 2), (2, 0), (1, 3), (3, 1)])
        got[3], rest = lax.optimization_barrier((got[3], rest))
    sums = [a.astype(jnp.float32) + b.astype(jnp.float32) for a, b in zip(kept, got)]
    got = [
        sent(s[1].astype(jnp.bfloat16), axis, way[0]) for s, axis, way in zip(sums, AXES, WAYS)
    ]
    return [s[0] + b.astype(jnp.float32) for s, b in zip(sums, got)], rest


def scatter_rest(parts):
    columns = []
    for half, axis in ((0, "b"), (1, "a")):
        got = sent(parts[2 * half + 1].astype(jnp.bfloat16), axis, far)
        pair = parts[2 * half] + got.astype(jnp.float32)
        got = sent(pair[1].astype(jnp.bfloat16), axis, near)
        columns.append(pair[0] + got.astype(jnp.float32))
    column = jnp.concatenate(columns, axis=-1)
    rounded = column.astype(jnp.bfloat16)
    total = column[0]
    for k in (3, 1, 2):
        got = sent(rounded[k], "z", DISTANCES[k])
        total = total + got.astype(jnp.float32)
    return total


def replica_sum(anchor, fragment, which, after, before):
    after, anchor, fragment = lax.optimization_barrier((after, anchor, fragment))
    anchor_f = lax.dynamic_index_in_dim(anchor, which[0], 0, keepdims=False)
    local_f = lax.dynamic_index_in_dim(fragment, which[0], 0, keepdims=False)
    partner = lax.ppermute(local_f, "replica", [(0, 1), (1, 0), (2, 3), (3, 2)])
    before, partner = lax.optimization_barrier((before, partner))
    pair = (anchor_f - local_f.astype(jnp.float32)) + (anchor_f - partner.astype(jnp.float32))
    return pair, after, before


def outer_kernel(which_ref, fragment, anchor, moment, pair, rest, *outs):
    new_fragment, new_anchor, new_moment = outs
    which = which_ref[0]
    new_fragment[...] = fragment[...]
    new_anchor[...] = anchor[...]
    new_moment[...] = moment[...]
    mean = (pair[...] + rest[...]) * (1.0 / REPLICAS)
    moved = 0.9 * moment[which] + mean
    stepped = anchor[which] - 0.7 * (mean + 0.9 * moved)
    new_moment[which] = moved
    new_anchor[which] = stepped
    local = fragment[which].astype(jnp.float32)
    new_fragment[which] = (0.5 * local + 0.5 * stepped).astype(jnp.bfloat16)


def outer_call(which, fragment, anchor, moment, pair, rest):
    vmem = pl.BlockSpec(memory_space=pltpu.VMEM)
    return pl.pallas_call(
        outer_kernel,
        out_shape=[jax.ShapeDtypeStruct(a.shape, a.dtype) for a in (fragment, anchor, moment)],
        in_specs=[pl.BlockSpec(memory_space=pltpu.SMEM)] + [vmem] * 5,
        out_specs=[vmem] * 3,
        cost_estimate=pl.CostEstimate(flops=0, bytes_accessed=3 * 1024 * 1024, transcendentals=0),
    )(which, fragment, anchor, moment, pair, rest)


def label_table():
    index = lax.axis_index("fsdp")
    x, y, z = (coordinate(index, axis) for axis in ("x", "y", "z"))
    of_x = [[p * STRIDE["x"] for p in labels(x)] for labels in (near_first, far_first)]
    of_y = [[p * STRIDE["y"] for p in labels(y)] for labels in (near_first, far_first)]
    of_z = [[along_z(z, k, core) * STRIDE["z"] for k in DISTANCES] for core in range(CORES)]
    first = jnp.stack([jnp.stack(row) for row in of_x + of_y + of_z[:1]])
    second = jnp.stack([jnp.stack(row) for row in of_y + of_x + of_z[1:]])
    even = lax.axis_index("replica") % CORES == 0
    return jnp.where(even, first, second).astype(jnp.int32)


def body(
    patches, inner_weights, inner_moment, fragment_replica, anchor, outer_moment, fragment_index
):
    inputs, weights, moment = patches[0], inner_weights[0], inner_moment[0]
    fragment = fragment_replica[0]
    tokens = inputs.shape[0] * lax.axis_size("fsdp")
    table = label_table()
    which = fragment_index % FRAGS
    rest = outer = None
    for turn in range(INNER):
        kept, other = gather_rest(gather_columns(weights.astype(jnp.bfloat16)))
        if turn == 0:
            pair, other[0], other[3] = replica_sum(anchor, fragment, which, other[0], other[3])
        else:
            other[0], pair = lax.optimization_barrier((other[0], pair))
            outer = outer_call(which, fragment, anchor, outer_moment, pair, rest)
            other[3], outer = lax.optimization_barrier((other[3], outer))
        kept, other = turn_call(table, inputs, kept, other)
        if turn == 0:
            kept, pair = lax.optimization_barrier((kept, pair))
            parts, rest = scatter_first(kept, other, pair)
        else:
            parts, _ = scatter_first(kept, other)
        grad = scatter_rest(parts) * (1.0 / tokens)
        mixed = 0.9 * moment + 0.1 * grad
        weights = weights * (1.0 - 0.01 * 0.1) - 0.01 * soft_sign(mixed)
        moment = 0.99 * moment + 0.01 * grad
    new_fragment, new_anchor, new_outer_moment = outer
    return (weights[None], moment[None], new_fragment[None], new_anchor, new_outer_moment)


def solution(mesh):
    return jax.shard_map(
        body,
        mesh=mesh,
        in_specs=(
            P("replica", "fsdp", None),
            P("replica", "fsdp", None),
            P("replica", "fsdp", None),
            P("replica", None, "fsdp", None),
            P(None, "fsdp", None),
            P(None, "fsdp", None),
            P(),
        ),
        out_specs=(
            P("replica", "fsdp", None),
            P("replica", "fsdp", None),
            P("replica", None, "fsdp", None),
            P(None, "fsdp", None),
            P(None, "fsdp", None),
        ),
        check_vma=False,
    )
```

```python
import jax
import jax.numpy as jnp
from jax import lax
from jax.experimental import pallas as pl
from jax.experimental.pallas import tpu as pltpu
from jax.sharding import PartitionSpec as P

IMAGE = 256
INNER = 2
FRAGS = 4
REPLICAS = 4
CORES = 2
DISTANCES = (0, 1, 3, 2)
SIDE = 4
CHUNKS = 6
STRIDE = {"x": 1, "z": 4, "y": 16}


def coordinate(index, axis):
    return (index // STRIDE[axis]) % SIDE


def near(place):
    return place + 1 - 2 * (place % 2)


def far(place):
    return SIDE - 1 - place


def near_first(place):
    return [place, near(place), far(place), near(far(place))]


def far_first(place):
    return [place, far(place), near(place), far(near(place))]


def axis_of(name, replica):
    if name == "z":
        return name
    return "x" if (name == "a") == (replica % CORES == 0) else "y"


def sent(value, axis, to):
    pairs = []
    for replica in range(REPLICAS):
        real = axis_of(axis, replica)
        for source in range(SIDE**3):
            place = coordinate(source, real)
            goal = (place + to) % SIDE if axis == "z" else to(place)
            target = source + (goal - place) * STRIDE[real]
            pairs.append((replica * SIDE**3 + source, replica * SIDE**3 + target))
    return lax.ppermute(value, ("replica", "fsdp"), pairs)


def swapped(value):
    return lax.ppermute(value, "replica", [(0, 1), (1, 0), (2, 3), (3, 2)])


def soft_sign(value):
    return value / jnp.sqrt(value * value + 1e-06)


def split_bf16(value):
    high = value.astype(jnp.bfloat16)
    low = (value - high.astype(jnp.float32)).astype(jnp.bfloat16)
    return high, low


def dot(a, b):
    return jnp.dot(a, b, preferred_element_type=jnp.float32)


def dot_first(a, b):
    return lax.dot_general(a, b, (((0,), (0,)), ((), ())), preferred_element_type=jnp.float32)


def blocks(table_ref, rows):
    found = []
    for half in range(2):
        for part in range(2):
            for i in range(SIDE):
                for j in range(SIDE // 2):
                    for k in range(SIDE):
                        first = table_ref[2 * half + part, i]
                        second = table_ref[2 * (1 - half), 2 * part + j]
                        block = first + second + table_ref[4, k]
                        found.append((half, part, (i, j, k), pl.multiple_of(block * rows, 32)))
    return found


def turn_kernel(table_ref, core_ref, inputs_hbm, *refs):
    kept_in, other_in, far_kept_in, far_other_in = refs[0:2], refs[2:4], refs[4], refs[5:7]
    kept_out, other_out, far_kept_out, far_other_out = refs[7:9], refs[9:11], refs[11], refs[12]
    inputs, weights, product, mixed, grad, sems = refs[13:]
    tokens, width = inputs.shape
    step = width // CHUNKS
    rows, head = far_kept_in.shape[4:]
    places = blocks(table_ref, rows)
    columns = [
        pl.ds(pl.multiple_of(core_ref[0] * head, head), head),
        pl.ds(pl.multiple_of((1 - core_ref[0]) * head, head), head),
    ]

    def fetch(c):
        part = pl.ds(pl.multiple_of(c * step, step), step)
        return pltpu.make_async_copy(inputs_hbm.at[:, part], inputs.at[:, part], sems.at[c])

    for c in range(CHUNKS):
        fetch(c).start()
    for half, part, (i, j, k), row in places:
        if half == 0:
            source = kept_in[part][i, j, k] if i < 2 else other_in[part][i - 2, j, k]
        else:
            source = far_kept_in[part, i, j, k] if i < 2 else far_other_in[part][i - 2, j, k]
        weights[pl.ds(row, rows), columns[half]] = source
    output_part = weights[:, head:]
    gram_high, gram_low = split_bf16(dot_first(output_part, output_part))
    product[...] = jnp.zeros_like(product)

    @pl.loop(0, CHUNKS)
    def _(c):
        fetch(c).wait()
        part = pl.ds(pl.multiple_of(c * step, step), step)
        product[...] += dot(inputs[:, part], weights[part, :])

    gram = jnp.concatenate([gram_high, gram_low], axis=0)
    squares = jnp.zeros((head, head), jnp.float32)
    for image in range(tokens // IMAGE):
        span = slice(image * IMAGE, (image + 1) * IMAGE)
        rounded = product[span, :head].astype(jnp.bfloat16)
        projected = product[span, head:]
        following = pltpu.roll(projected, IMAGE - 1, 0)
        twice = jnp.concatenate([rounded, rounded], axis=1)
        back = projected - following + dot(twice, gram)
        hidden = rounded.astype(jnp.float32)
        mixed[span, :head] = back.astype(jnp.bfloat16)
        mixed[span, head:] = (hidden - pltpu.roll(hidden, 1, 0)).astype(jnp.bfloat16)
        squares = squares + dot_first(rounded, rounded)
    squares = jnp.concatenate(split_bf16(squares), axis=0)

    @pl.loop(0, CHUNKS)
    def _(c):
        part = pl.ds(pl.multiple_of(c * step, step), step)
        term = dot_first(inputs[:, part], mixed[...])
        output_rows = weights[part, head:]
        extra = dot(jnp.concatenate([output_rows, output_rows], axis=1), squares)
        grad[part, :head] = term[:, :head].astype(jnp.bfloat16)
        grad[part, head:] = (term[:, head:] + extra).astype(jnp.bfloat16)

    for half, part, (i, j, k), row in places:
        block = grad[pl.ds(row, rows), columns[half]]
        if half == 0:
            out = kept_out if i < 2 else other_out
            out[part][i % 2, j, k] = block
        else:
            out = far_kept_out if i < 2 else far_other_out
            out[part, i % 2, j, k] = block


def turn_call(table, core, inputs, kept, other, far_kept, far_other):
    tokens, width = inputs.shape
    head = far_kept.shape[-1]
    out = jax.ShapeDtypeStruct(kept[0].shape, jnp.bfloat16)
    far_out = jax.ShapeDtypeStruct(far_kept.shape, jnp.bfloat16)
    vmem = pl.BlockSpec(memory_space=pltpu.VMEM)
    smem = pl.BlockSpec(memory_space=pltpu.SMEM)
    outs = pl.pallas_call(
        turn_kernel,
        out_shape=[out] * 4 + [far_out] * 2,
        in_specs=[smem, smem, pl.BlockSpec(memory_space=pl.ANY)] + [vmem] * 7,
        out_specs=[vmem] * 6,
        scratch_shapes=[
            pltpu.VMEM((tokens, width), jnp.bfloat16),
            pltpu.VMEM((width, 2 * head), jnp.bfloat16),
            pltpu.VMEM((tokens, 2 * head), jnp.float32),
            pltpu.VMEM((tokens, 2 * head), jnp.bfloat16),
            pltpu.VMEM((width, 2 * head), jnp.bfloat16),
            pltpu.SemaphoreType.DMA((CHUNKS,)),
        ],
        compiler_params=pltpu.CompilerParams(vmem_limit_bytes=48 * 1024 * 1024),
        cost_estimate=pl.CostEstimate(
            flops=8 * tokens * width * head, bytes_accessed=2 * tokens * width, transcendentals=0
        ),
    )(table, core, inputs, *kept, *other, far_kept, *far_other)
    return outs[:2], outs[2:4], outs[4], outs[5]


WAYS = ((near, far), (far, near))


def gather(rounded):
    column = jnp.stack([rounded] + [sent(rounded, "z", -k) for k in DISTANCES[1:]])
    pair = jnp.stack([column, sent(column, "b", near)])
    parts = [pair, sent(pair, "b", far)]
    first = [sent(p, "a", way[0]) for p, way in zip(parts, WAYS)]
    kept = [jnp.stack(both) for both in zip(parts, first)]
    other = [sent(p, "a", way[1]) for p, way in zip(kept, WAYS)]
    return kept, other


def scatter_sum(kept, other, far_kept, far_other, pair=None):
    got_other, got_kept = swapped(far_other), swapped(far_kept)
    both = [jnp.stack([other[p], got_other[p]], axis=3) for p in range(2)]
    got = [sent(b, "a", way[1]) for b, way in zip(both, WAYS)]
    rest = None
    if pair is not None:
        rest = lax.ppermute(pair, "replica", [(0, 2), (2, 0), (1, 3), (3, 1)])
        got[1], rest = lax.optimization_barrier((got[1], rest))
    sums = [
        jnp.stack([kept[p], got_kept[p]], axis=3).astype(jnp.float32) + got[p].astype(jnp.float32)
        for p in range(2)
    ]
    got = [sent(v[1].astype(jnp.bfloat16), "a", way[0]) for v, way in zip(sums, WAYS)]
    sums = [v[0] + b.astype(jnp.float32) for v, b in zip(sums, got)]
    got = sent(sums[1].astype(jnp.bfloat16), "b", far)
    level = sums[0] + got.astype(jnp.float32)
    got = sent(level[1].astype(jnp.bfloat16), "b", near)
    column = level[0] + got.astype(jnp.float32)
    rounded = column.astype(jnp.bfloat16)
    total = column[0]
    for k in (3, 1, 2):
        total = total + sent(rounded[k], "z", DISTANCES[k]).astype(jnp.float32)
    return total, rest


def replica_sum(anchor, fragment, which, after, before):
    after, anchor, fragment = lax.optimization_barrier((after, anchor, fragment))
    anchor_f = lax.dynamic_index_in_dim(anchor, which[0], 0, keepdims=False)
    local_f = lax.dynamic_index_in_dim(fragment, which[0], 0, keepdims=False)
    partner = swapped(local_f)
    before, partner = lax.optimization_barrier((before, partner))
    pair = (anchor_f - local_f.astype(jnp.float32)) + (anchor_f - partner.astype(jnp.float32))
    return pair, after, before


def outer_kernel(which_ref, fragment, anchor, moment, pair, rest, *outs):
    new_fragment, new_anchor, new_moment = outs
    which = which_ref[0]
    new_fragment[...] = fragment[...]
    new_anchor[...] = anchor[...]
    new_moment[...] = moment[...]
    mean = (pair[...] + rest[...]) * (1.0 / REPLICAS)
    moved = 0.9 * moment[which] + mean
    stepped = anchor[which] - 0.7 * (mean + 0.9 * moved)
    new_moment[which] = moved
    new_anchor[which] = stepped
    local = fragment[which].astype(jnp.float32)
    new_fragment[which] = (0.5 * local + 0.5 * stepped).astype(jnp.bfloat16)


def outer_call(which, fragment, anchor, moment, pair, rest):
    vmem = pl.BlockSpec(memory_space=pltpu.VMEM)
    return pl.pallas_call(
        outer_kernel,
        out_shape=[jax.ShapeDtypeStruct(a.shape, a.dtype) for a in (fragment, anchor, moment)],
        in_specs=[pl.BlockSpec(memory_space=pltpu.SMEM)] + [vmem] * 5,
        out_specs=[vmem] * 3,
        cost_estimate=pl.CostEstimate(flops=0, bytes_accessed=3 * 1024 * 1024, transcendentals=0),
    )(which, fragment, anchor, moment, pair, rest)


def label_table():
    index = lax.axis_index("fsdp")
    x, y, z = (coordinate(index, axis) for axis in ("x", "y", "z"))
    of_x = [[p * STRIDE["x"] for p in labels(x)] for labels in (near_first, far_first)]
    of_y = [[p * STRIDE["y"] for p in labels(y)] for labels in (near_first, far_first)]
    of_z = [(z + k) % SIDE * STRIDE["z"] for k in DISTANCES]
    first = jnp.stack([jnp.stack(row) for row in of_x + of_y + [of_z]])
    second = jnp.stack([jnp.stack(row) for row in of_y + of_x + [of_z]])
    even = lax.axis_index("replica") % CORES == 0
    return jnp.where(even, first, second).astype(jnp.int32)


def halves(whole, core):
    middle = whole.shape[1] // 2
    left, right = whole[:, :middle], whole[:, middle:]
    return jnp.where(core == 0, left, right), jnp.where(core == 0, right, left)


def body(
    patches, inner_weights, inner_moment, fragment_replica, anchor, outer_moment, fragment_index
):
    inputs = patches[0]
    fragment = fragment_replica[0]
    tokens = inputs.shape[0] * lax.axis_size("fsdp")
    table = label_table()
    core = lax.axis_index("replica") % CORES
    core_array = core.astype(jnp.int32).reshape(1)
    which = fragment_index % FRAGS
    own, far_half = zip(halves(inner_weights[0], core), halves(inner_moment[0], core))
    got = swapped(jnp.stack(far_half))
    weights, moment = (jnp.stack([own[n], got[n]]) for n in range(2))
    rest = outer = None
    for turn in range(INNER):
        kept, other = gather(weights.astype(jnp.bfloat16))
        far_kept = swapped(jnp.stack([p[:, :, :, 1] for p in kept]))
        if turn == 0:
            pair, other[0], other[1] = replica_sum(anchor, fragment, which, other[0], other[1])
        else:
            other[0], pair = lax.optimization_barrier((other[0], pair))
            outer = outer_call(which, fragment, anchor, outer_moment, pair, rest)
            other[1], outer = lax.optimization_barrier((other[1], outer))
        far_other = [swapped(p[:, :, :, 1]) for p in other]
        kept, other = ([p[:, :, :, 0] for p in parts] for parts in (kept, other))
        outs = turn_call(table, core_array, inputs, kept, other, far_kept, far_other)
        if turn == 0:
            outs, pair = lax.optimization_barrier((outs, pair))
            grad, rest = scatter_sum(*outs, pair)
        else:
            grad, _ = scatter_sum(*outs)
        grad = grad * (1.0 / tokens)
        mixed = 0.9 * moment + 0.1 * grad
        weights = weights * (1.0 - 0.01 * 0.1) - 0.01 * soft_sign(mixed)
        moment = 0.99 * moment + 0.01 * grad
    state = jnp.stack([weights, moment])
    mine, got = state[:, 0], swapped(state[:, 1])
    left, right = jnp.where(core == 0, mine, got), jnp.where(core == 0, got, mine)
    state = jnp.concatenate([left, right], axis=-1)
    new_fragment, new_anchor, new_outer_moment = outer
    return (state[:1], state[1:], new_fragment[None], new_anchor, new_outer_moment)


def solution(mesh):
    return jax.shard_map(
        body,
        mesh=mesh,
        in_specs=(
            P("replica", "fsdp", None),
            P("replica", "fsdp", None),
            P("replica", "fsdp", None),
            P("replica", None, "fsdp", None),
            P(None, "fsdp", None),
            P(None, "fsdp", None),
            P(),
        ),
        out_specs=(
            P("replica", "fsdp", None),
            P("replica", "fsdp", None),
            P("replica", None, "fsdp", None),
            P(None, "fsdp", None),
            P(None, "fsdp", None),
        ),
        check_vma=False,
    )
```

```python
import jax
import jax.numpy as jnp
from jax import lax
from jax.experimental import pallas as pl
from jax.experimental.pallas import tpu as pltpu
from jax.sharding import PartitionSpec as P

IMAGE = 256
INNER = 2
FRAGS = 4
REPLICAS = 4
SIDE = 4
CHUNKS = 6
STRIDE = {"x": 1, "z": 4, "y": 16}


def coordinate(index, axis):
    return (index // STRIDE[axis]) % SIDE


def near(place):
    return place + 1 - 2 * (place % 2)


def far(place):
    return SIDE - 1 - place


def near_first(place):
    return [place, near(place), far(place), near(far(place))]


def far_first(place):
    return [place, far(place), near(place), far(near(place))]


def sent(value, axis, to):
    pairs = []
    for source in range(SIDE**3):
        place = coordinate(source, axis)
        pairs.append((source, source + (to(place) - place) * STRIDE[axis]))
    return lax.ppermute(value, "fsdp", pairs)


def soft_sign(value):
    return value / jnp.sqrt(value * value + 1e-06)


def split_bf16(value):
    high = value.astype(jnp.bfloat16)
    low = (value - high.astype(jnp.float32)).astype(jnp.bfloat16)
    return high, low


def dot(a, b):
    return jnp.dot(a, b, preferred_element_type=jnp.float32)


def dot_first(a, b):
    return lax.dot_general(a, b, (((0,), (0,)), ((), ())), preferred_element_type=jnp.float32)


def block_slots():
    for part in range(4):
        for i in range(SIDE):
            for j in range(SIDE // 2):
                for k in range(SIDE):
                    yield part, (i, j, k)


def block_rows(rows):
    index = lax.axis_index("fsdp")
    x, y, z = (coordinate(index, axis) for axis in ("x", "y", "z"))
    x, y = ([jnp.stack(labels(p)) for labels in (near_first, far_first)] for p in (x, y))
    z = (z + jnp.arange(SIDE)) % SIDE
    found = []
    for part in range(4):
        output, back = part // 2, part % 2
        first = (y if output else x)[back]
        second = (x if output else y)[0][2 * back : 2 * back + 2]
        first = (first * STRIDE["y" if output else "x"])[:, None, None]
        second = (second * STRIDE["x" if output else "y"])[None, :, None]
        found.append(first + second + (z * STRIDE["z"])[None, None, :])
    return (jnp.stack(found) * rows).reshape(-1).astype(jnp.int32)


def turn_kernel(rows_ref, inputs_hbm, *refs):
    kept_in, other_in = refs[0:4], refs[4:8]
    kept_out, other_out = refs[8:12], refs[12:16]
    inputs, weights, product, mixed, grad, sems = refs[16:]
    tokens, width = inputs.shape
    step = width // CHUNKS
    rows, head = kept_in[0].shape[3:]
    places = []
    for number, (part, slot) in enumerate(block_slots()):
        row = pl.multiple_of(rows_ref[number], 32)
        half = slice(part // 2 * head, (part // 2 + 1) * head)
        places.append((part, slot, (pl.ds(row, rows), half)))

    def fetch(c):
        part = pl.ds(pl.multiple_of(c * step, step), step)
        return pltpu.make_async_copy(inputs_hbm.at[:, part], inputs.at[:, part], sems.at[c])

    for c in range(CHUNKS):
        fetch(c).start()
    for part, (i, j, k), block in places:
        weights[block] = kept_in[part][i, j, k] if i < 2 else other_in[part][i - 2, j, k]
    output_part = weights[:, head:]
    gram_high, gram_low = split_bf16(dot_first(output_part, output_part))
    product[...] = jnp.zeros_like(product)

    @pl.loop(0, CHUNKS)
    def _(c):
        fetch(c).wait()
        part = pl.ds(pl.multiple_of(c * step, step), step)
        product[...] += dot(inputs[:, part], weights[part, :])

    gram = jnp.concatenate([gram_high, gram_low], axis=0)
    squares = jnp.zeros((head, head), jnp.float32)
    for image in range(tokens // IMAGE):
        span = slice(image * IMAGE, (image + 1) * IMAGE)
        rounded = product[span, :head].astype(jnp.bfloat16)
        projected = product[span, head:]
        following = pltpu.roll(projected, IMAGE - 1, 0)
        twice = jnp.concatenate([rounded, rounded], axis=1)
        back = projected - following + dot(twice, gram)
        hidden = rounded.astype(jnp.float32)
        mixed[span, :head] = back.astype(jnp.bfloat16)
        mixed[span, head:] = (hidden - pltpu.roll(hidden, 1, 0)).astype(jnp.bfloat16)
        squares = squares + dot_first(rounded, rounded)
    squares = jnp.concatenate(split_bf16(squares), axis=0)

    @pl.loop(0, CHUNKS)
    def _(c):
        part = pl.ds(pl.multiple_of(c * step, step), step)
        term = dot_first(inputs[:, part], mixed[...])
        output_rows = weights[part, head:]
        extra = dot(jnp.concatenate([output_rows, output_rows], axis=1), squares)
        grad[part, :head] = term[:, :head].astype(jnp.bfloat16)
        grad[part, head:] = (term[:, head:] + extra).astype(jnp.bfloat16)

    for part, (i, j, k), block in places:
        if i < 2:
            kept_out[part][i, j, k] = grad[block]
        else:
            other_out[part][i - 2, j, k] = grad[block]


def turn_call(first_rows, inputs, kept, other):
    tokens, width = inputs.shape
    shape = kept[0].shape
    head = shape[-1]
    out = jax.ShapeDtypeStruct(shape, jnp.bfloat16)
    vmem = pl.BlockSpec(memory_space=pltpu.VMEM)
    outs = pl.pallas_call(
        turn_kernel,
        out_shape=[out] * 8,
        in_specs=[pl.BlockSpec(memory_space=pltpu.SMEM), pl.BlockSpec(memory_space=pl.ANY)]
        + [vmem] * 8,
        out_specs=[vmem] * 8,
        scratch_shapes=[
            pltpu.VMEM((tokens, width), jnp.bfloat16),
            pltpu.VMEM((width, 2 * head), jnp.bfloat16),
            pltpu.VMEM((tokens, 2 * head), jnp.float32),
            pltpu.VMEM((tokens, 2 * head), jnp.bfloat16),
            pltpu.VMEM((width, 2 * head), jnp.bfloat16),
            pltpu.SemaphoreType.DMA((CHUNKS,)),
        ],
        compiler_params=pltpu.CompilerParams(vmem_limit_bytes=44 * 1024 * 1024),
        cost_estimate=pl.CostEstimate(
            flops=8 * tokens * width * head, bytes_accessed=2 * tokens * width, transcendentals=0
        ),
    )(first_rows, inputs, *kept, *other)
    return outs[:4], outs[4:]


WAYS = ((near, far), (far, near), (near, far), (far, near))
AXES = ("x", "x", "y", "y")
ORDER = (1, 3, 0, 2)


def gather_columns(rounded, first_work=None, next_work=None):
    head = rounded.shape[1] // 2
    parts = [rounded]
    for k in range(1, SIDE):
        parts.append(sent(rounded, "z", lambda place, k=k: (place - k) % SIDE))
    if first_work is not None:
        parts[3], parts[1], done = first_work(parts[3], parts[1])
    column = jnp.stack(parts)
    halves = [column[:, :, :head], column[:, :, head:]]
    pairs = [jnp.stack([h, sent(h, axis, near)]) for h, axis in zip(halves, ("y", "x"))]
    wide = [jnp.concatenate([p, sent(p, axis, far)]) for p, axis in zip(pairs, ("y", "x"))]
    if next_work is not None:
        _, wide[1], done = next_work(column, wide[1])
    return wide, done


def gather_rest(wide):
    parts = [wide[0][:2], wide[0][2:], wide[1][:2], wide[1][2:]]
    first = [sent(p, axis, way[0]) for p, axis, way in zip(parts, AXES, WAYS)]
    kept = [jnp.stack(both) for both in zip(parts, first)]
    other = [sent(p, axis, way[1]) for p, axis, way in zip(kept, AXES, WAYS)]
    return kept, other


def scatter_first(kept, other):
    parts = [None] * 4
    sums = [None] * 4
    for n in ORDER:
        got = sent(other[n], AXES[n], WAYS[n][1])
        sums[n] = kept[n].astype(jnp.float32) + got.astype(jnp.float32)
    for n in ORDER:
        got = sent(sums[n][1].astype(jnp.bfloat16), AXES[n], WAYS[n][0])
        parts[n] = sums[n][0] + got.astype(jnp.float32)
    return parts


def scatter_rest(parts):
    columns = []
    for half, axis in ((0, "y"), (1, "x")):
        got = sent(parts[2 * half + 1].astype(jnp.bfloat16), axis, far)
        pair = parts[2 * half] + got.astype(jnp.float32)
        got = sent(pair[1].astype(jnp.bfloat16), axis, near)
        columns.append(pair[0] + got.astype(jnp.float32))
    column = jnp.concatenate(columns, axis=-1)
    rounded = column.astype(jnp.bfloat16)
    total = column[0]
    for k in range(1, SIDE):
        got = sent(rounded[k], "z", lambda place, k=k: (place + k) % SIDE)
        total = total + got.astype(jnp.float32)
    return total


def placed(work, *operands):
    def beside(after, before):
        values = lax.optimization_barrier((after, *operands))
        result = work(*values[1:])
        before, result = lax.optimization_barrier((before, result))
        return values[0], before, result

    return beside


def pair_sum(anchor, fragment, which):
    anchor_f = lax.dynamic_index_in_dim(anchor, which[0], 0, keepdims=False)
    local_f = lax.dynamic_index_in_dim(fragment, which[0], 0, keepdims=False)
    partner = lax.ppermute(local_f, "replica", [(0, 1), (1, 0), (2, 3), (3, 2)])
    return (anchor_f - local_f.astype(jnp.float32)) + (anchor_f - partner.astype(jnp.float32))


def other_pair(pair):
    return pair, lax.ppermute(pair, "replica", [(0, 2), (2, 0), (1, 3), (3, 1)])


def outer_kernel(which_ref, fragment, anchor, moment, pair, rest, *outs):
    new_fragment, new_anchor, new_moment = outs
    which = which_ref[0]
    new_fragment[...] = fragment[...]
    new_anchor[...] = anchor[...]
    new_moment[...] = moment[...]
    mean = (pair[...] + rest[...]) * (1.0 / REPLICAS)
    moved = 0.9 * moment[which] + mean
    stepped = anchor[which] - 0.7 * (mean + 0.9 * moved)
    new_moment[which] = moved
    new_anchor[which] = stepped
    local = fragment[which].astype(jnp.float32)
    new_fragment[which] = (0.5 * local + 0.5 * stepped).astype(jnp.bfloat16)


def outer_call(which, fragment, anchor, moment, pair, rest):
    vmem = pl.BlockSpec(memory_space=pltpu.VMEM)
    return pl.pallas_call(
        outer_kernel,
        out_shape=[jax.ShapeDtypeStruct(a.shape, a.dtype) for a in (fragment, anchor, moment)],
        in_specs=[pl.BlockSpec(memory_space=pltpu.SMEM)] + [vmem] * 5,
        out_specs=[vmem] * 3,
        cost_estimate=pl.CostEstimate(flops=0, bytes_accessed=3 * 1024 * 1024, transcendentals=0),
    )(which, fragment, anchor, moment, pair, rest)


def body(
    patches, inner_weights, inner_moment, fragment_replica, anchor, outer_moment, fragment_index
):
    inputs, weights, moment = patches[0], inner_weights[0], inner_moment[0]
    fragment = fragment_replica[0]
    tokens = inputs.shape[0] * lax.axis_size("fsdp")
    first_rows = block_rows(inner_weights.shape[1])
    which = fragment_index % FRAGS
    outer = None
    for turn in range(INNER):
        rounded = weights.astype(jnp.bfloat16)
        if turn == 0:
            work = placed(pair_sum, anchor, fragment, which)
            wide, outer = gather_columns(rounded, first_work=work)
        else:
            wide, outer = gather_columns(rounded, next_work=placed(other_pair, outer))
        kept, other = gather_rest(wide)
        if turn == 1:
            work = placed(outer_call, which, fragment, anchor, outer_moment, *outer)
            other[0], other[3], outer = work(other[0], other[3])
        kept, other = turn_call(first_rows, inputs, kept, other)
        grad = scatter_rest(scatter_first(kept, other)) * (1.0 / tokens)
        mixed = 0.9 * moment + 0.1 * grad
        weights = weights * (1.0 - 0.01 * 0.1) - 0.01 * soft_sign(mixed)
        moment = 0.99 * moment + 0.01 * grad
    new_fragment, new_anchor, new_outer_moment = outer
    return (weights[None], moment[None], new_fragment[None], new_anchor, new_outer_moment)


def solution(mesh):
    return jax.shard_map(
        body,
        mesh=mesh,
        in_specs=(
            P("replica", "fsdp", None),
            P("replica", "fsdp", None),
            P("replica", "fsdp", None),
            P("replica", None, "fsdp", None),
            P(None, "fsdp", None),
            P(None, "fsdp", None),
            P(),
        ),
        out_specs=(
            P("replica", "fsdp", None),
            P("replica", "fsdp", None),
            P("replica", None, "fsdp", None),
            P(None, "fsdp", None),
            P(None, "fsdp", None),
        ),
        check_vma=False,
    )
```

```python
import jax
import jax.numpy as jnp
from jax import lax
from jax.experimental import pallas as pl
from jax.experimental.pallas import tpu as pltpu
from jax.sharding import PartitionSpec as P

IMAGE = 256
INNER = 2
FRAGS = 4
REPLICAS = 4
ORDER = (1, 0, 3, 2)
SIDE = 4
CHUNKS = 6
STRIDE = {"x": 1, "z": 4, "y": 16}


def coordinate(index, axis):
    return (index // STRIDE[axis]) % SIDE


def near(place):
    return place + 1 - 2 * (place % 2)


def far(place):
    return SIDE - 1 - place


def near_first(place):
    return [place, near(place), far(place), near(far(place))]


def far_first(place):
    return [place, far(place), near(place), far(near(place))]


def sent(value, axis, to):
    pairs = []
    for source in range(SIDE**3):
        place = coordinate(source, axis)
        pairs.append((source, source + (to(place) - place) * STRIDE[axis]))
    return lax.ppermute(value, "fsdp", pairs)


def soft_sign(value):
    return value / jnp.sqrt(value * value + 1e-06)


def split_bf16(value):
    high = value.astype(jnp.bfloat16)
    low = (value - high.astype(jnp.float32)).astype(jnp.bfloat16)
    return high, low


def dot(a, b):
    return jnp.dot(a, b, preferred_element_type=jnp.float32)


def dot_first(a, b):
    return lax.dot_general(a, b, (((0,), (0,)), ((), ())), preferred_element_type=jnp.float32)


def block_slots():
    for part in range(4):
        for i in range(SIDE):
            for j in range(SIDE // 2):
                for k in range(SIDE):
                    yield part, (i, j, k)


def block_rows(rows):
    index = lax.axis_index("fsdp")
    x, y, z = (coordinate(index, axis) for axis in ("x", "y", "z"))
    x, y = ([jnp.stack(labels(p)) for labels in (near_first, far_first)] for p in (x, y))
    z = (z + jnp.arange(SIDE)) % SIDE
    found = []
    for part in range(4):
        output, back = part // 2, part % 2
        first = (y if output else x)[back]
        second = (x if output else y)[0][2 * back : 2 * back + 2]
        first = (first * STRIDE["y" if output else "x"])[:, None, None]
        second = (second * STRIDE["x" if output else "y"])[None, :, None]
        found.append(first + second + (z * STRIDE["z"])[None, None, :])
    return (jnp.stack(found) * rows).reshape(-1).astype(jnp.int32)


def in_order(parts):
    return [parts[n] for n in ORDER]


def turn_kernel(rows_ref, inputs_hbm, *refs):
    kept_in, other_in = in_order(refs[0:4]), in_order(refs[4:8])
    kept_out, other_out = refs[8:12], refs[12:16]
    inputs, weights, product, mixed, grad, sems = refs[16:]
    tokens, width = inputs.shape
    step = width // CHUNKS
    rows, head = kept_in[0].shape[3:]
    places = []
    for number, (part, slot) in enumerate(block_slots()):
        row = pl.multiple_of(rows_ref[number], 32)
        half = slice(part // 2 * head, (part // 2 + 1) * head)
        places.append((part, slot, (pl.ds(row, rows), half)))

    def fetch(c):
        part = pl.ds(pl.multiple_of(c * step, step), step)
        return pltpu.make_async_copy(inputs_hbm.at[:, part], inputs.at[:, part], sems.at[c])

    for c in range(CHUNKS):
        fetch(c).start()
    for part, (i, j, k), block in places:
        weights[block] = kept_in[part][i, j, k] if i < 2 else other_in[part][i - 2, j, k]
    output_part = weights[:, head:]
    gram_high, gram_low = split_bf16(dot_first(output_part, output_part))
    product[...] = jnp.zeros_like(product)

    @pl.loop(0, CHUNKS)
    def _(c):
        fetch(c).wait()
        part = pl.ds(pl.multiple_of(c * step, step), step)
        product[...] += dot(inputs[:, part], weights[part, :])

    gram = jnp.concatenate([gram_high, gram_low], axis=0)
    squares = jnp.zeros((head, head), jnp.float32)
    for image in range(tokens // IMAGE):
        span = slice(image * IMAGE, (image + 1) * IMAGE)
        rounded = product[span, :head].astype(jnp.bfloat16)
        projected = product[span, head:]
        following = pltpu.roll(projected, IMAGE - 1, 0)
        twice = jnp.concatenate([rounded, rounded], axis=1)
        back = projected - following + dot(twice, gram)
        hidden = rounded.astype(jnp.float32)
        mixed[span, :head] = back.astype(jnp.bfloat16)
        mixed[span, head:] = (hidden - pltpu.roll(hidden, 1, 0)).astype(jnp.bfloat16)
        squares = squares + dot_first(rounded, rounded)
    squares = jnp.concatenate(split_bf16(squares), axis=0)

    @pl.loop(0, CHUNKS)
    def _(c):
        part = pl.ds(pl.multiple_of(c * step, step), step)
        term = dot_first(inputs[:, part], mixed[...])
        output_rows = weights[part, head:]
        extra = dot(jnp.concatenate([output_rows, output_rows], axis=1), squares)
        grad[part, :head] = term[:, :head].astype(jnp.bfloat16)
        grad[part, head:] = (term[:, head:] + extra).astype(jnp.bfloat16)

    for part, (i, j, k), block in places:
        if i < 2:
            kept_out[part][i, j, k] = grad[block]
        else:
            other_out[part][i - 2, j, k] = grad[block]


def turn_call(first_rows, inputs, kept, other):
    tokens, width = inputs.shape
    shape = kept[0].shape
    head = shape[-1]
    out = jax.ShapeDtypeStruct(shape, jnp.bfloat16)
    vmem = pl.BlockSpec(memory_space=pltpu.VMEM)
    outs = pl.pallas_call(
        turn_kernel,
        out_shape=[out] * 8,
        in_specs=[pl.BlockSpec(memory_space=pltpu.SMEM), pl.BlockSpec(memory_space=pl.ANY)]
        + [vmem] * 8,
        out_specs=[vmem] * 8,
        scratch_shapes=[
            pltpu.VMEM((tokens, width), jnp.bfloat16),
            pltpu.VMEM((width, 2 * head), jnp.bfloat16),
            pltpu.VMEM((tokens, 2 * head), jnp.float32),
            pltpu.VMEM((tokens, 2 * head), jnp.bfloat16),
            pltpu.VMEM((width, 2 * head), jnp.bfloat16),
            pltpu.SemaphoreType.DMA((CHUNKS,)),
        ],
        compiler_params=pltpu.CompilerParams(vmem_limit_bytes=44 * 1024 * 1024),
        cost_estimate=pl.CostEstimate(
            flops=8 * tokens * width * head, bytes_accessed=2 * tokens * width, transcendentals=0
        ),
    )(first_rows, inputs, *in_order(kept), *in_order(other))
    return outs[:4], outs[4:]


WAYS = ((near, far), (far, near), (near, far), (far, near))
AXES = ("x", "x", "y", "y")


def gather_columns(rounded, work=None):
    head = rounded.shape[1] // 2
    parts = [rounded]
    for k in range(1, SIDE):
        parts.append(sent(rounded, "z", lambda place, k=k: (place - k) % SIDE))
    done = None
    if work is not None:
        parts[3], parts[1], done = work(parts[3], parts[1])
    column = jnp.stack(parts)
    halves = [column[:, :, :head], column[:, :, head:]]
    pairs = [jnp.stack([h, sent(h, axis, near)]) for h, axis in zip(halves, ("y", "x"))]
    far_pairs = [sent(p, axis, far) for p, axis in zip(pairs, ("y", "x"))]
    pairs = lax.optimization_barrier(pairs)
    wide = [jnp.concatenate(both) for both in zip(pairs, far_pairs)]
    return wide, done


def gather_rest(wide, work=None):
    parts = [wide[0][:2], wide[0][2:], wide[1][:2], wide[1][2:]]
    done = None
    first = [sent(p, axis, way[0]) for p, axis, way in zip(parts, AXES, WAYS)]
    if work is not None:
        first[0], first[1], done = work(first[0], first[1])
    kept = [jnp.stack(both) for both in zip(parts, first)]
    other = [sent(p, axis, way[1]) for p, axis, way in zip(kept, AXES, WAYS)]
    return kept, other, done


def scatter_first(kept, other):
    parts = []
    for n in range(4):
        got = sent(other[n], AXES[n], WAYS[n][1])
        total = kept[n].astype(jnp.float32) + got.astype(jnp.float32)
        got = sent(total[1].astype(jnp.bfloat16), AXES[n], WAYS[n][0])
        parts.append(total[0] + got.astype(jnp.float32))
    return parts


def scatter_rest(parts):
    columns = []
    for half, axis in ((0, "y"), (1, "x")):
        got = sent(parts[2 * half + 1].astype(jnp.bfloat16), axis, far)
        pair = got.astype(jnp.float32) + parts[2 * half]
        got = sent(pair[1].astype(jnp.bfloat16), axis, near)
        columns.append(pair[0] + got.astype(jnp.float32))
    column = jnp.concatenate(columns, axis=-1)
    rounded = column.astype(jnp.bfloat16)
    total = column[0]
    for k in range(1, SIDE):
        got = sent(rounded[k], "z", lambda place, k=k: (place + k) % SIDE)
        total = total + got.astype(jnp.float32)
    return total


def placed(work, *operands):
    def beside(after, before):
        values = lax.optimization_barrier((after, *operands))
        result = work(*values[1:])
        before, result = lax.optimization_barrier((before, result))
        return values[0], before, result

    return beside


def pair_sum(anchor, fragment, which):
    anchor_f = lax.dynamic_index_in_dim(anchor, which[0], 0, keepdims=False)
    local_f = lax.dynamic_index_in_dim(fragment, which[0], 0, keepdims=False)
    partner = lax.ppermute(local_f, "replica", [(0, 1), (1, 0), (2, 3), (3, 2)])
    return (anchor_f - local_f.astype(jnp.float32)) + (anchor_f - partner.astype(jnp.float32))


def other_pair(pair):
    return pair, lax.ppermute(pair, "replica", [(0, 2), (2, 0), (1, 3), (3, 1)])


def outer_kernel(which_ref, fragment, anchor, moment, pair, rest, *outs):
    new_fragment, new_anchor, new_moment = outs
    which = which_ref[0]
    new_fragment[...] = fragment[...]
    new_anchor[...] = anchor[...]
    new_moment[...] = moment[...]
    mean = (pair[...] + rest[...]) * (1.0 / REPLICAS)
    moved = 0.9 * moment[which] + mean
    stepped = anchor[which] - 0.7 * (mean + 0.9 * moved)
    new_moment[which] = moved
    new_anchor[which] = stepped
    local = fragment[which].astype(jnp.float32)
    new_fragment[which] = (0.5 * local + 0.5 * stepped).astype(jnp.bfloat16)


def outer_call(which, fragment, anchor, moment, pair, rest):
    vmem = pl.BlockSpec(memory_space=pltpu.VMEM)
    return pl.pallas_call(
        outer_kernel,
        out_shape=[jax.ShapeDtypeStruct(a.shape, a.dtype) for a in (fragment, anchor, moment)],
        in_specs=[pl.BlockSpec(memory_space=pltpu.SMEM)] + [vmem] * 5,
        out_specs=[vmem] * 3,
        cost_estimate=pl.CostEstimate(flops=0, bytes_accessed=3 * 1024 * 1024, transcendentals=0),
    )(which, fragment, anchor, moment, pair, rest)


def body(
    patches, inner_weights, inner_moment, fragment_replica, anchor, outer_moment, fragment_index
):
    inputs, weights, moment = patches[0], inner_weights[0], inner_moment[0]
    fragment = fragment_replica[0]
    tokens = inputs.shape[0] * lax.axis_size("fsdp")
    first_rows = block_rows(inner_weights.shape[1])
    which = fragment_index % FRAGS
    outer = None
    for turn in range(INNER):
        rounded = weights.astype(jnp.bfloat16)
        if turn == 0:
            wide, outer = gather_columns(rounded, placed(pair_sum, anchor, fragment, which))
            kept, other, _ = gather_rest(wide)
        else:
            wide, _ = gather_columns(rounded)
            kept, other, outer = gather_rest(wide, placed(other_pair, outer))
            work = placed(outer_call, which, fragment, anchor, outer_moment, *outer)
            other[0], other[3], outer = work(other[0], other[3])
        kept, other = turn_call(first_rows, inputs, kept, other)
        grad = scatter_rest(scatter_first(kept, other)) * (1.0 / tokens)
        mixed = 0.9 * moment + 0.1 * grad
        weights = weights * (1.0 - 0.01 * 0.1) - 0.01 * soft_sign(mixed)
        moment = 0.99 * moment + 0.01 * grad
    new_fragment, new_anchor, new_outer_moment = outer
    return (weights[None], moment[None], new_fragment[None], new_anchor, new_outer_moment)


def solution(mesh):
    return jax.shard_map(
        body,
        mesh=mesh,
        in_specs=(
            P("replica", "fsdp", None),
            P("replica", "fsdp", None),
            P("replica", "fsdp", None),
            P("replica", None, "fsdp", None),
            P(None, "fsdp", None),
            P(None, "fsdp", None),
            P(),
        ),
        out_specs=(
            P("replica", "fsdp", None),
            P("replica", "fsdp", None),
            P("replica", None, "fsdp", None),
            P(None, "fsdp", None),
            P(None, "fsdp", None),
        ),
        check_vma=False,
    )
```

```python
import jax
import jax.numpy as jnp
from jax import lax
from jax.experimental import pallas as pl
from jax.experimental.pallas import tpu as pltpu
from jax.sharding import PartitionSpec as P

IMAGE = 256
INNER = 2
FRAGS = 4
REPLICAS = 4
ORDER = (1, 0, 3, 2)
SIDE = 4
CHUNKS = 3
STRIDE = {"x": 1, "z": 4, "y": 16}


def coordinate(index, axis):
    return (index // STRIDE[axis]) % SIDE


def near(place):
    return place + 1 - 2 * (place % 2)


def far(place):
    return SIDE - 1 - place


def near_first(place):
    return [place, near(place), far(place), near(far(place))]


def far_first(place):
    return [place, far(place), near(place), far(near(place))]


def sent(value, axis, to):
    pairs = []
    for source in range(SIDE**3):
        place = coordinate(source, axis)
        pairs.append((source, source + (to(place) - place) * STRIDE[axis]))
    return lax.ppermute(value, "fsdp", pairs)


def soft_sign(value):
    return value / jnp.sqrt(value * value + 1e-06)


def split_bf16(value):
    high = value.astype(jnp.bfloat16)
    low = (value - high.astype(jnp.float32)).astype(jnp.bfloat16)
    return high, low


def dot(a, b):
    return jnp.dot(a, b, preferred_element_type=jnp.float32)


def dot_first(a, b):
    return lax.dot_general(a, b, (((0,), (0,)), ((), ())), preferred_element_type=jnp.float32)


def block_slots():
    for part in range(4):
        for i in range(SIDE):
            for j in range(SIDE // 2):
                for k in range(SIDE):
                    yield part, (i, j, k)


def block_rows(rows):
    index = lax.axis_index("fsdp")
    x, y, z = (coordinate(index, axis) for axis in ("x", "y", "z"))
    x, y = ([jnp.stack(labels(p)) for labels in (near_first, far_first)] for p in (x, y))
    z = (z + jnp.arange(SIDE)) % SIDE
    found = []
    for part in range(4):
        output, back = part // 2, part % 2
        first = (y if output else x)[back]
        second = (x if output else y)[0][2 * back : 2 * back + 2]
        first = (first * STRIDE["y" if output else "x"])[:, None, None]
        second = (second * STRIDE["x" if output else "y"])[None, :, None]
        found.append(first + second + (z * STRIDE["z"])[None, None, :])
    return (jnp.stack(found) * rows).reshape(-1).astype(jnp.int32)


def in_order(parts):
    return [parts[n] for n in ORDER]


def turn_kernel(rows_ref, inputs_hbm, *refs):
    kept_in, other_in = in_order(refs[0:4]), in_order(refs[4:8])
    kept_out, other_out = refs[8:12], refs[12:16]
    inputs, weights, product, mixed, grad, sems = refs[16:]
    tokens, width = inputs.shape
    step = width // CHUNKS
    rows, head = kept_in[0].shape[3:]
    places = []
    for number, (part, slot) in enumerate(block_slots()):
        row = pl.multiple_of(rows_ref[number], 32)
        half = slice(part // 2 * head, (part // 2 + 1) * head)
        places.append((part, slot, (pl.ds(row, rows), half)))

    def fetch(c):
        part = pl.ds(pl.multiple_of(c * step, step), step)
        return pltpu.make_async_copy(inputs_hbm.at[:, part], inputs.at[:, part], sems.at[c])

    for c in range(CHUNKS):
        fetch(c).start()
    for part, (i, j, k), block in places:
        weights[block] = kept_in[part][i, j, k] if i < 2 else other_in[part][i - 2, j, k]
    output_part = weights[:, head:]
    gram_high, gram_low = split_bf16(dot_first(output_part, output_part))
    product[...] = jnp.zeros_like(product)

    @pl.loop(0, CHUNKS)
    def _(c):
        fetch(c).wait()
        part = pl.ds(pl.multiple_of(c * step, step), step)
        product[...] += dot(inputs[:, part], weights[part, :])

    gram = jnp.concatenate([gram_high, gram_low], axis=0)
    squares = jnp.zeros((head, head), jnp.float32)
    for image in range(tokens // IMAGE):
        span = slice(image * IMAGE, (image + 1) * IMAGE)
        rounded = product[span, :head].astype(jnp.bfloat16)
        projected = product[span, head:]
        following = pltpu.roll(projected, IMAGE - 1, 0)
        twice = jnp.concatenate([rounded, rounded], axis=1)
        back = projected - following + dot(twice, gram)
        hidden = rounded.astype(jnp.float32)
        mixed[span, :head] = back.astype(jnp.bfloat16)
        mixed[span, head:] = (hidden - pltpu.roll(hidden, 1, 0)).astype(jnp.bfloat16)
        squares = squares + dot_first(rounded, rounded)
    squares = jnp.concatenate(split_bf16(squares), axis=0)

    @pl.loop(0, CHUNKS)
    def _(c):
        part = pl.ds(pl.multiple_of(c * step, step), step)
        term = dot_first(inputs[:, part], mixed[...])
        output_rows = weights[part, head:]
        extra = dot(jnp.concatenate([output_rows, output_rows], axis=1), squares)
        grad[part, :head] = term[:, :head].astype(jnp.bfloat16)
        grad[part, head:] = (term[:, head:] + extra).astype(jnp.bfloat16)

    for part, (i, j, k), block in places:
        if i < 2:
            kept_out[part][i, j, k] = grad[block]
        else:
            other_out[part][i - 2, j, k] = grad[block]


def turn_call(first_rows, inputs, kept, other):
    tokens, width = inputs.shape
    shape = kept[0].shape
    head = shape[-1]
    out = jax.ShapeDtypeStruct(shape, jnp.bfloat16)
    vmem = pl.BlockSpec(memory_space=pltpu.VMEM)
    outs = pl.pallas_call(
        turn_kernel,
        out_shape=[out] * 8,
        in_specs=[pl.BlockSpec(memory_space=pltpu.SMEM), pl.BlockSpec(memory_space=pl.ANY)]
        + [vmem] * 8,
        out_specs=[vmem] * 8,
        scratch_shapes=[
            pltpu.VMEM((tokens, width), jnp.bfloat16),
            pltpu.VMEM((width, 2 * head), jnp.bfloat16),
            pltpu.VMEM((tokens, 2 * head), jnp.float32),
            pltpu.VMEM((tokens, 2 * head), jnp.bfloat16),
            pltpu.VMEM((width, 2 * head), jnp.bfloat16),
            pltpu.SemaphoreType.DMA((CHUNKS,)),
        ],
        compiler_params=pltpu.CompilerParams(vmem_limit_bytes=44 * 1024 * 1024),
        cost_estimate=pl.CostEstimate(
            flops=8 * tokens * width * head, bytes_accessed=2 * tokens * width, transcendentals=0
        ),
    )(first_rows, inputs, *in_order(kept), *in_order(other))
    return outs[:4], outs[4:]


WAYS = ((near, far), (far, near), (near, far), (far, near))
AXES = ("x", "x", "y", "y")


def gather_columns(rounded):
    head = rounded.shape[1] // 2
    parts = [rounded]
    for k in range(1, SIDE):
        parts.append(sent(rounded, "z", lambda place, k=k: (place - k) % SIDE))
    column = jnp.stack(parts)
    halves = [column[:, :, :head], column[:, :, head:]]
    pairs = [jnp.stack([h, sent(h, axis, near)]) for h, axis in zip(halves, ("y", "x"))]
    far_pairs = [sent(p, axis, far) for p, axis in zip(pairs, ("y", "x"))]
    pairs = lax.optimization_barrier(pairs)
    wide = [jnp.concatenate(both) for both in zip(pairs, far_pairs)]
    return wide


def gather_rest(wide):
    parts = [wide[0][:2], wide[0][2:], wide[1][:2], wide[1][2:]]
    first = [sent(p, axis, way[0]) for p, axis, way in zip(parts, AXES, WAYS)]
    kept = [jnp.stack(both) for both in zip(parts, first)]
    other = [sent(p, axis, way[1]) for p, axis, way in zip(kept, AXES, WAYS)]
    return kept, other


def scatter_first(kept, other):
    parts = []
    for n in range(4):
        got = sent(other[n], AXES[n], WAYS[n][1])
        total = kept[n].astype(jnp.float32) + got.astype(jnp.float32)
        got = sent(total[1].astype(jnp.bfloat16), AXES[n], WAYS[n][0])
        parts.append(total[0] + got.astype(jnp.float32))
    return parts


def scatter_rest(parts):
    columns = []
    for half, axis in ((0, "y"), (1, "x")):
        got = sent(parts[2 * half + 1].astype(jnp.bfloat16), axis, far)
        pair = got.astype(jnp.float32) + parts[2 * half]
        got = sent(pair[1].astype(jnp.bfloat16), axis, near)
        columns.append(pair[0] + got.astype(jnp.float32))
    column = jnp.concatenate(columns, axis=-1)
    rounded = column.astype(jnp.bfloat16)
    total = column[0]
    for k in range(1, SIDE):
        got = sent(rounded[k], "z", lambda place, k=k: (place + k) % SIDE)
        total = total + got.astype(jnp.float32)
    return total


def placed(work, *operands):
    def beside(after, before):
        values = lax.optimization_barrier((after, *operands))
        result = work(*values[1:])
        before, result = lax.optimization_barrier((before, result))
        return values[0], before, result

    return beside


def pair_sum(anchor, fragment, which):
    anchor_f = lax.dynamic_index_in_dim(anchor, which[0], 0, keepdims=False)
    local_f = lax.dynamic_index_in_dim(fragment, which[0], 0, keepdims=False)
    partner = lax.ppermute(local_f, "replica", [(0, 1), (1, 0), (2, 3), (3, 2)])
    return (anchor_f - local_f.astype(jnp.float32)) + (anchor_f - partner.astype(jnp.float32))


def other_pair(pair):
    return pair, lax.ppermute(pair, "replica", [(0, 2), (2, 0), (1, 3), (3, 1)])


def outer_kernel(which_ref, fragment, anchor, moment, pair, rest, *outs):
    new_fragment, new_anchor, new_moment = outs
    which = which_ref[0]
    new_fragment[...] = fragment[...]
    new_anchor[...] = anchor[...]
    new_moment[...] = moment[...]
    mean = (pair[...] + rest[...]) * (1.0 / REPLICAS)
    moved = 0.9 * moment[which] + mean
    stepped = anchor[which] - 0.7 * (mean + 0.9 * moved)
    new_moment[which] = moved
    new_anchor[which] = stepped
    local = fragment[which].astype(jnp.float32)
    new_fragment[which] = (0.5 * local + 0.5 * stepped).astype(jnp.bfloat16)


def outer_call(which, fragment, anchor, moment, pair, rest):
    vmem = pl.BlockSpec(memory_space=pltpu.VMEM)
    return pl.pallas_call(
        outer_kernel,
        out_shape=[jax.ShapeDtypeStruct(a.shape, a.dtype) for a in (fragment, anchor, moment)],
        in_specs=[pl.BlockSpec(memory_space=pltpu.SMEM)] + [vmem] * 5,
        out_specs=[vmem] * 3,
        cost_estimate=pl.CostEstimate(flops=0, bytes_accessed=3 * 1024 * 1024, transcendentals=0),
    )(which, fragment, anchor, moment, pair, rest)


def body(
    patches, inner_weights, inner_moment, fragment_replica, anchor, outer_moment, fragment_index
):
    inputs, weights, moment = patches[0], inner_weights[0], inner_moment[0]
    fragment = fragment_replica[0]
    tokens = inputs.shape[0] * lax.axis_size("fsdp")
    first_rows = block_rows(inner_weights.shape[1])
    which = fragment_index % FRAGS
    outer = None
    for turn in range(INNER):
        kept, other = gather_rest(gather_columns(weights.astype(jnp.bfloat16)))
        if turn == 0:
            work = placed(pair_sum, anchor, fragment, which)
        else:
            work = placed(outer_call, which, fragment, anchor, outer_moment, *outer)
        other[0], other[3], outer = work(other[0], other[3])
        if turn == 0:
            outer = other_pair(outer)
        kept, other = turn_call(first_rows, inputs, kept, other)
        if turn == 0:
            kept, outer = lax.optimization_barrier((kept, outer))
        grad = scatter_rest(scatter_first(kept, other)) * (1.0 / tokens)
        mixed = 0.9 * moment + 0.1 * grad
        weights = weights * (1.0 - 0.01 * 0.1) - 0.01 * soft_sign(mixed)
        moment = 0.99 * moment + 0.01 * grad
    new_fragment, new_anchor, new_outer_moment = outer
    return (weights[None], moment[None], new_fragment[None], new_anchor, new_outer_moment)


def solution(mesh):
    return jax.shard_map(
        body,
        mesh=mesh,
        in_specs=(
            P("replica", "fsdp", None),
            P("replica", "fsdp", None),
            P("replica", "fsdp", None),
            P("replica", None, "fsdp", None),
            P(None, "fsdp", None),
            P(None, "fsdp", None),
            P(),
        ),
        out_specs=(
            P("replica", "fsdp", None),
            P("replica", "fsdp", None),
            P("replica", None, "fsdp", None),
            P(None, "fsdp", None),
            P(None, "fsdp", None),
        ),
        check_vma=False,
    )
```

```python
import jax
import jax.numpy as jnp
from jax import lax
from jax.experimental import pallas as pl
from jax.experimental.pallas import tpu as pltpu
from jax.sharding import PartitionSpec as P

IMAGE = 256
INNER = 2
FRAGS = 4
REPLICAS = 4
ORDER = (1, 0, 3, 2)
SIDE = 4
CHUNKS = 3
STRIDE = {"x": 1, "z": 4, "y": 16}


def coordinate(index, axis):
    return (index // STRIDE[axis]) % SIDE


def near(place):
    return place + 1 - 2 * (place % 2)


def far(place):
    return SIDE - 1 - place


def near_first(place):
    return [place, near(place), far(place), near(far(place))]


def far_first(place):
    return [place, far(place), near(place), far(near(place))]


def sent(value, axis, to):
    pairs = []
    for source in range(SIDE**3):
        place = coordinate(source, axis)
        pairs.append((source, source + (to(place) - place) * STRIDE[axis]))
    return lax.ppermute(value, "fsdp", pairs)


def soft_sign(value):
    return value / jnp.sqrt(value * value + 1e-06)


def split_bf16(value):
    high = value.astype(jnp.bfloat16)
    low = (value - high.astype(jnp.float32)).astype(jnp.bfloat16)
    return high, low


def dot(a, b):
    return jnp.dot(a, b, preferred_element_type=jnp.float32)


def dot_first(a, b):
    return lax.dot_general(a, b, (((0,), (0,)), ((), ())), preferred_element_type=jnp.float32)


def block_slots():
    for part in range(4):
        for i in range(SIDE):
            for j in range(SIDE // 2):
                for k in range(SIDE):
                    yield part, (i, j, k)


def block_rows(rows):
    index = lax.axis_index("fsdp")
    x, y, z = (coordinate(index, axis) for axis in ("x", "y", "z"))
    x, y = ([jnp.stack(labels(p)) for labels in (near_first, far_first)] for p in (x, y))
    z = (z + jnp.arange(SIDE)) % SIDE
    found = []
    for part in range(4):
        output, back = part // 2, part % 2
        first = (y if output else x)[back]
        second = (x if output else y)[0][2 * back : 2 * back + 2]
        first = (first * STRIDE["y" if output else "x"])[:, None, None]
        second = (second * STRIDE["x" if output else "y"])[None, :, None]
        found.append(first + second + (z * STRIDE["z"])[None, None, :])
    return (jnp.stack(found) * rows).reshape(-1).astype(jnp.int32)


def in_order(parts):
    return [parts[n] for n in ORDER]


def turn_kernel(rows_ref, inputs_hbm, *refs):
    kept_in, other_in = in_order(refs[0:4]), in_order(refs[4:8])
    kept_out, other_out = refs[8:12], refs[12:16]
    inputs, weights, product, mixed, grad, sems = refs[16:]
    tokens, width = inputs.shape
    step = width // CHUNKS
    rows, head = kept_in[0].shape[3:]
    places = []
    for number, (part, slot) in enumerate(block_slots()):
        row = pl.multiple_of(rows_ref[number], 32)
        half = slice(part // 2 * head, (part // 2 + 1) * head)
        places.append((part, slot, (pl.ds(row, rows), half)))

    def fetch(c):
        part = pl.ds(pl.multiple_of(c * step, step), step)
        return pltpu.make_async_copy(inputs_hbm.at[:, part], inputs.at[:, part], sems.at[c])

    for c in range(CHUNKS):
        fetch(c).start()
    for part, (i, j, k), block in places:
        weights[block] = kept_in[part][i, j, k] if i < 2 else other_in[part][i - 2, j, k]
    output_part = weights[:, head:]
    gram_high, gram_low = split_bf16(dot_first(output_part, output_part))
    product[...] = jnp.zeros_like(product)

    @pl.loop(0, CHUNKS)
    def _(c):
        fetch(c).wait()
        part = pl.ds(pl.multiple_of(c * step, step), step)
        product[...] += dot(inputs[:, part], weights[part, :])

    gram = jnp.concatenate([gram_high, gram_low], axis=0)
    squares = jnp.zeros((head, head), jnp.float32)
    for image in range(tokens // IMAGE):
        span = slice(image * IMAGE, (image + 1) * IMAGE)
        rounded = product[span, :head].astype(jnp.bfloat16)
        projected = product[span, head:]
        following = pltpu.roll(projected, IMAGE - 1, 0)
        twice = jnp.concatenate([rounded, rounded], axis=1)
        back = projected - following + dot(twice, gram)
        hidden = rounded.astype(jnp.float32)
        mixed[span, :head] = back.astype(jnp.bfloat16)
        mixed[span, head:] = (hidden - pltpu.roll(hidden, 1, 0)).astype(jnp.bfloat16)
        squares = squares + dot_first(rounded, rounded)
    squares = jnp.concatenate(split_bf16(squares), axis=0)

    @pl.loop(0, CHUNKS)
    def _(c):
        part = pl.ds(pl.multiple_of(c * step, step), step)
        term = dot_first(inputs[:, part], mixed[...])
        output_rows = weights[part, head:]
        extra = dot(jnp.concatenate([output_rows, output_rows], axis=1), squares)
        grad[part, :head] = term[:, :head].astype(jnp.bfloat16)
        grad[part, head:] = (term[:, head:] + extra).astype(jnp.bfloat16)

    for part, (i, j, k), block in places:
        if i < 2:
            kept_out[part][i, j, k] = grad[block]
        else:
            other_out[part][i - 2, j, k] = grad[block]


def turn_call(first_rows, inputs, kept, other):
    tokens, width = inputs.shape
    shape = kept[0].shape
    head = shape[-1]
    out = jax.ShapeDtypeStruct(shape, jnp.bfloat16)
    vmem = pl.BlockSpec(memory_space=pltpu.VMEM)
    outs = pl.pallas_call(
        turn_kernel,
        out_shape=[out] * 8,
        in_specs=[pl.BlockSpec(memory_space=pltpu.SMEM), pl.BlockSpec(memory_space=pl.ANY)]
        + [vmem] * 8,
        out_specs=[vmem] * 8,
        scratch_shapes=[
            pltpu.VMEM((tokens, width), jnp.bfloat16),
            pltpu.VMEM((width, 2 * head), jnp.bfloat16),
            pltpu.VMEM((tokens, 2 * head), jnp.float32),
            pltpu.VMEM((tokens, 2 * head), jnp.bfloat16),
            pltpu.VMEM((width, 2 * head), jnp.bfloat16),
            pltpu.SemaphoreType.DMA((CHUNKS,)),
        ],
        compiler_params=pltpu.CompilerParams(vmem_limit_bytes=44 * 1024 * 1024),
        cost_estimate=pl.CostEstimate(
            flops=8 * tokens * width * head, bytes_accessed=2 * tokens * width, transcendentals=0
        ),
    )(first_rows, inputs, *in_order(kept), *in_order(other))
    return outs[:4], outs[4:]


WAYS = ((near, far), (far, near), (near, far), (far, near))
AXES = ("x", "x", "y", "y")


def gather_columns(rounded):
    head = rounded.shape[1] // 2
    parts = [rounded]
    for k in range(1, SIDE):
        parts.append(sent(rounded, "z", lambda place, k=k: (place - k) % SIDE))
    column = jnp.stack(parts)
    halves = [column[:, :, :head], column[:, :, head:]]
    pairs = [jnp.stack([h, sent(h, axis, near)]) for h, axis in zip(halves, ("y", "x"))]
    far_pairs = [sent(p, axis, far) for p, axis in zip(pairs, ("y", "x"))]
    pairs = lax.optimization_barrier(pairs)
    wide = [jnp.concatenate(both) for both in zip(pairs, far_pairs)]
    return wide


def gather_rest(wide):
    parts = [wide[0][:2], wide[0][2:], wide[1][:2], wide[1][2:]]
    first = [sent(p, axis, way[0]) for p, axis, way in zip(parts, AXES, WAYS)]
    kept = [jnp.stack(both) for both in zip(parts, first)]
    other = [sent(p, axis, way[1]) for p, axis, way in zip(kept, AXES, WAYS)]
    return kept, other


def scatter_first(kept, other):
    parts = []
    for n in range(4):
        got = sent(other[n], AXES[n], WAYS[n][1])
        total = kept[n].astype(jnp.float32) + got.astype(jnp.float32)
        got = sent(total[1].astype(jnp.bfloat16), AXES[n], WAYS[n][0])
        parts.append(total[0] + got.astype(jnp.float32))
    return parts


def scatter_rest(parts):
    columns = []
    for half, axis in ((0, "y"), (1, "x")):
        got = sent(parts[2 * half + 1].astype(jnp.bfloat16), axis, far)
        pair = got.astype(jnp.float32) + parts[2 * half]
        got = sent(pair[1].astype(jnp.bfloat16), axis, near)
        columns.append(pair[0] + got.astype(jnp.float32))
    column = jnp.concatenate(columns, axis=-1)
    rounded = column.astype(jnp.bfloat16)
    total = column[0]
    for k in (2, 1, 3):
        got = sent(rounded[k], "z", lambda place, k=k: (place + k) % SIDE)
        total = total + got.astype(jnp.float32)
    return total


def placed(work, *operands):
    def beside(after, before):
        values = lax.optimization_barrier((after, *operands))
        result = work(*values[1:])
        before, result = lax.optimization_barrier((before, result))
        return values[0], before, result

    return beside


def pair_sum(anchor, fragment, which):
    anchor_f = lax.dynamic_index_in_dim(anchor, which[0], 0, keepdims=False)
    local_f = lax.dynamic_index_in_dim(fragment, which[0], 0, keepdims=False)
    partner = lax.ppermute(local_f, "replica", [(0, 1), (1, 0), (2, 3), (3, 2)])
    return (anchor_f - local_f.astype(jnp.float32)) + (anchor_f - partner.astype(jnp.float32))


def other_pair(pair):
    return pair, lax.ppermute(pair, "replica", [(0, 2), (2, 0), (1, 3), (3, 1)])


def outer_kernel(which_ref, fragment, anchor, moment, pair, rest, *outs):
    new_fragment, new_anchor, new_moment = outs
    which = which_ref[0]
    new_fragment[...] = fragment[...]
    new_anchor[...] = anchor[...]
    new_moment[...] = moment[...]
    mean = (pair[...] + rest[...]) * (1.0 / REPLICAS)
    moved = 0.9 * moment[which] + mean
    stepped = anchor[which] - 0.7 * (mean + 0.9 * moved)
    new_moment[which] = moved
    new_anchor[which] = stepped
    local = fragment[which].astype(jnp.float32)
    new_fragment[which] = (0.5 * local + 0.5 * stepped).astype(jnp.bfloat16)


def outer_call(which, fragment, anchor, moment, pair, rest):
    vmem = pl.BlockSpec(memory_space=pltpu.VMEM)
    return pl.pallas_call(
        outer_kernel,
        out_shape=[jax.ShapeDtypeStruct(a.shape, a.dtype) for a in (fragment, anchor, moment)],
        in_specs=[pl.BlockSpec(memory_space=pltpu.SMEM)] + [vmem] * 5,
        out_specs=[vmem] * 3,
        cost_estimate=pl.CostEstimate(flops=0, bytes_accessed=3 * 1024 * 1024, transcendentals=0),
    )(which, fragment, anchor, moment, pair, rest)


def body(
    patches, inner_weights, inner_moment, fragment_replica, anchor, outer_moment, fragment_index
):
    inputs, weights, moment = patches[0], inner_weights[0], inner_moment[0]
    fragment = fragment_replica[0]
    tokens = inputs.shape[0] * lax.axis_size("fsdp")
    first_rows = block_rows(inner_weights.shape[1])
    which = fragment_index % FRAGS
    outer = None
    for turn in range(INNER):
        kept, other = gather_rest(gather_columns(weights.astype(jnp.bfloat16)))
        if turn == 0:
            work = placed(pair_sum, anchor, fragment, which)
        else:
            work = placed(outer_call, which, fragment, anchor, outer_moment, *outer)
        other[0], other[3], outer = work(other[0], other[3])
        if turn == 0:
            outer = other_pair(outer)
        kept, other = turn_call(first_rows, inputs, kept, other)
        if turn == 0:
            kept, outer = lax.optimization_barrier((kept, outer))
        grad = scatter_rest(scatter_first(kept, other)) * (1.0 / tokens)
        mixed = 0.9 * moment + 0.1 * grad
        weights = weights * (1.0 - 0.01 * 0.1) - 0.01 * soft_sign(mixed)
        moment = 0.99 * moment + 0.01 * grad
    new_fragment, new_anchor, new_outer_moment = outer
    return (weights[None], moment[None], new_fragment[None], new_anchor, new_outer_moment)


def solution(mesh):
    return jax.shard_map(
        body,
        mesh=mesh,
        in_specs=(
            P("replica", "fsdp", None),
            P("replica", "fsdp", None),
            P("replica", "fsdp", None),
            P("replica", None, "fsdp", None),
            P(None, "fsdp", None),
            P(None, "fsdp", None),
            P(),
        ),
        out_specs=(
            P("replica", "fsdp", None),
            P("replica", "fsdp", None),
            P("replica", None, "fsdp", None),
            P(None, "fsdp", None),
            P(None, "fsdp", None),
        ),
        check_vma=False,
    )
```
